128 devices in a mesh: segment: 4 (over x_lo, core), space: 32 (over y, x_hi, z).
Axes of the slice: x: 4 (x_hi: 2, x_lo: 2; x = x_hi * 2 + x_lo), y: 4, z: 4, core: 2. Of those that a mesh axis runs over, the one named last changes fastest.
Arguments:
- state: float32 [2, 5, 2, 256, 64], P(None, None, None, 'space'), may hold values from -6 to 6
- noise: float32 [2, 4, 2, 256, 64], P(None, None, None, 'space'), may hold values from -6 to 6
- land_sea: int32 [256, 64], P('space'), may hold values 0 or 1
- observed_truth: float32 [2, 5, 2, 256, 64], P(None, None, None, 'space', 'segment'), may hold values from -6 to 6
- embed_w: float32 [7, 256], replicated, may hold values from -2 to 2
- fine_weight_kernels: bfloat16 [2, 6912, 128], replicated, may hold values from -0.078125 to 0.078125
- merge_w: bfloat16 [512, 256], replicated, may hold values from -0.25 to 0.25
- coarse_w: bfloat16 [4, 6912, 256], replicated, may hold values from -0.078125 to 0.078125
- expand_w: bfloat16 [256, 512], replicated, may hold values from -0.375 to 0.375
- head_w: bfloat16 [128, 5], replicated, may hold values from -0.5 to 0.5
Outputs:
- member_prediction: float32 [2, 4, 5, 2, 256, 64], P(None, None, None, None, 'space', 'segment')
- crps: float32 [2, 5, 2, 256, 64], P(None, None, None, 'space', 'segment')
The draws below stay inside these ranges and needn't reach their ends.
All inputs are finite; a program needn't handle non-finite values. No bound on the sum of `land_sea` on one device may be relied on, other than what follows from the above.
Results may differ from the reference program's by a relative error of at most 0.0022.
Values may be sent and summed in bfloat16 or wider, within the bound.
No kernel may reach another device: no remote copies, remote signals or barrier semaphores. Data moves between devices by JAX's collectives and lax.ppermute only.
A program may use at most 192 MiB of HBM per device.

```python
import jax
import jax.numpy as jnp
from jax import lax

C1 = 128
C2 = 256
VARS = 5
LEV = 2
MEMBERS = 4
MICRO = 2
LON = 64
NLAT = 256


def plant(values, own_key, least, high):
    longest = values.shape.index(max(values.shape))
    spots = []
    for shift in (0, 1):
        where = [jax.random.randint(jax.random.fold_in(own_key, axis), (), 0, length) for axis, length in enumerate(values.shape)]
        where[longest] = (where[longest] + shift) % values.shape[longest]
        spots.append(tuple(where))
    return values.at[spots[0]].set(least).at[spots[1]].set(high)


def level_of(stream_key, shape, shards, smallest, high):
    loudness, own = 1.0, jax.random.fold_in(stream_key, 6)
    for dim, shards_of in shards:
        draws = jnp.exp(jax.random.uniform(jax.random.fold_in(own, dim), (shards_of,), jnp.float32, smallest / len(shards), high / len(shards)))
        loudness = loudness * jnp.repeat(draws, shape[dim] // shards_of).reshape([-1 if axis == dim else 1 for axis in range(len(shape))])
    return loudness


def normal_values(own_key, shape, width, reach, split=(), dtype=jnp.bfloat16):
    array = width * jax.random.normal(own_key, shape, jnp.float32)
    if split:
        array = array * level_of(own_key, shape, split, -0.22, 0.18)
    return jnp.clip(array, -reach, reach).astype(dtype)


def setup_inputs(seed: int = 0) -> dict:
    seeds = jax.random.split(jax.random.key(seed), 11)
    state = normal_values(seeds[0], (MICRO, VARS, LEV, NLAT, LON), 1.0, 6.0, ((3, 32),), jnp.float32)
    noise = normal_values(seeds[1], (MICRO, MEMBERS, LEV, NLAT, LON), 1.0, 6.0, ((3, 32),), jnp.float32)
    land_sea = plant((jax.random.randint(seeds[2], (NLAT, LON), 0, 3) < 1).astype(jnp.int32), jax.random.fold_in(seeds[2], 1), 0, 1)
    observed_truth = normal_values(seeds[3], (MICRO, VARS, LEV, NLAT, LON), 1.0, 6.0, ((3, 32), (4, 4)), jnp.float32)
    embed_w = normal_values(seeds[4], (VARS + 2, C2), (VARS + 2) ** -0.5, 2.0, (), jnp.float32)
    fine_weight_kernels = normal_values(seeds[5], (2, 27 * C2, C1), (27 * C2) ** -0.5, 0.078125)
    merge_w = normal_values(seeds[6], (4 * C1, C2), (4 * C1) ** -0.5, 0.25)
    coarse_w = normal_values(seeds[7], (4, 27 * C2, C2), (27 * C2) ** -0.5, 0.078125)
    expand_w = normal_values(seeds[8], (C2, 4 * C1), C2 ** -0.5, 0.375)
    head_w = normal_values(seeds[9], (C1, VARS), C1 ** -0.5, 0.5)
    return {"state": state, "noise": noise, "land_sea": land_sea, "observed_truth": observed_truth, "embed_w": embed_w, "fine_weight_kernels": fine_weight_kernels, "merge_w": merge_w, "coarse_w": coarse_w, "expand_w": expand_w, "head_w": head_w}


def conv_member(padded, weight):
    span_z = padded.shape[0] - 2
    span_y = padded.shape[1] - 2
    span_x = padded.shape[2] - 2
    taps = [padded[depth:depth + span_z, north:north + span_y, east:east + span_x, :]
            for depth in range(3) for north in range(3) for east in range(3)]
    stacked = jnp.concatenate(taps, axis=-1)
    flat = stacked.reshape(span_z * span_y * span_x, stacked.shape[-1])
    result = jnp.dot(flat, weight, preferred_element_type=jnp.float32)
    return result.reshape(span_z, span_y, span_x, weight.shape[-1])


def conv_full(fields_in, weight):
    padded = jnp.pad(fields_in, ((0, 0), (1, 1), (1, 1), (1, 1), (0, 0)))
    return lax.map(lambda member: conv_member(member, weight), padded)


def embed_fields(state_m, noise_m, land_sea, embed_w):
    members = noise_m.shape[0]
    moved = jnp.transpose(state_m, (1, 2, 3, 0))
    base = jnp.broadcast_to(moved[None], (members,) + moved.shape)
    land = jnp.broadcast_to(land_sea.astype(jnp.float32)[None, None, :, :, None], noise_m.shape + (1,))
    feats = jnp.concatenate([base, noise_m[..., None], land], axis=-1)
    mixed = jnp.einsum("bzyxf,fc->bzyxc", feats, embed_w, precision=lax.Precision.HIGHEST)
    return jax.nn.gelu(mixed).astype(jnp.bfloat16)


def merge_patches(fine, merge_w):
    bsz, zsz, ysz, xsz, csz = fine.shape
    grouped = fine.reshape(bsz, zsz, ysz // 2, 2, xsz // 2, 2, csz).transpose(0, 1, 2, 4, 3, 5, 6)
    grouped = grouped.reshape(bsz, zsz, ysz // 2, xsz // 2, 4 * csz)
    return jax.nn.gelu(jnp.dot(grouped, merge_w, preferred_element_type=jnp.float32)).astype(jnp.bfloat16)


def expand_patches(coarse, expand_w):
    bsz, zsz, ysz, xsz, _ = coarse.shape
    narrow = expand_w.shape[1] // 4
    spread = jnp.dot(coarse, expand_w, preferred_element_type=jnp.float32).astype(jnp.bfloat16)
    spread = spread.reshape(bsz, zsz, ysz, xsz, 2, 2, narrow).transpose(0, 1, 2, 4, 3, 5, 6)
    return spread.reshape(bsz, zsz, 2 * ysz, 2 * xsz, narrow)


def residual_step(fields_in, conv_out):
    return (fields_in.astype(jnp.float32) + jax.nn.gelu(conv_out)).astype(jnp.bfloat16)


def head_term(decoded, head_w):
    return jnp.transpose(jnp.dot(decoded, head_w, preferred_element_type=jnp.float32), (0, 4, 1, 2, 3))


def probabilistic_skill_aggregate(pred, truth):
    members = pred.shape[0]
    skill = jnp.mean(jnp.abs(pred - truth[None]), axis=0)
    spread = jnp.sum(jnp.abs(pred[:, None] - pred[None, :]), axis=(0, 1)) / (2.0 * members * (members - 1))
    return skill - spread


def reference(state, noise, land_sea, observed_truth, embed_w, fine_weight_kernels, merge_w, coarse_w, expand_w, head_w):
    preds = []
    skill_entries = []
    for sample_count in range(MICRO):
        embedded = embed_fields(state[sample_count], noise[sample_count], land_sea, embed_w)
        skip = jax.nn.gelu(conv_full(embedded, fine_weight_kernels[0])).astype(jnp.bfloat16)
        coarse = merge_patches(skip, merge_w)
        for layer in range(4):
            coarse = residual_step(coarse, conv_full(coarse, coarse_w[layer]))
        upsampled = expand_patches(coarse, expand_w)
        combined_tensor = jnp.concatenate([upsampled, skip], axis=-1)
        decoded = jax.nn.gelu(conv_full(combined_tensor, fine_weight_kernels[1])).astype(jnp.bfloat16)
        pred = state[sample_count][None] + head_term(decoded, head_w)
        preds.append(pred)
        skill_entries.append(probabilistic_skill_aggregate(pred, observed_truth[sample_count]))
    return jnp.stack(preds), jnp.stack(skill_entries)
```

```python
import jax
import jax.numpy as jnp
from jax import lax
from jax.experimental import pallas as pl
from jax.experimental.pallas import tpu as pltpu
from jax.sharding import PartitionSpec as P

F32 = jnp.float32
BF16 = jnp.bfloat16
AXES = ("segment", "space")
SEGMENTS = 4
TILES = 32
GROUP = 4
VMEM_LIMIT = 60 * 1024 * 1024
R1 = 6
R2 = 8


def gelu(x):
    half = 0.5 * x
    t = jnp.tanh(x * (0.7978845608028654 + 0.035677408136300125 * (x * x)))
    return half + half * t


def nn(a, b):
    return lax.dot_general(a, b, (((1,), (0,)), ((), ())), preferred_element_type=F32)


def nt(a, b):
    return lax.dot_general(a, b, (((1,), (1,)), ((), ())), preferred_element_type=F32)


def iota(shape, dim):
    return lax.broadcasted_iota(jnp.int32, shape, dim)


def member_of(segment, space):
    return segment ^ (2 * ((space // GROUP) % 2))


def pack_kernel(state_ref, noise_ref, land_ref, out_ref, even_ref, odd_ref):
    member = member_of(lax.axis_index("segment"), lax.axis_index("space"))
    even_ref[...] = jnp.zeros_like(even_ref)
    odd_ref[...] = jnp.zeros_like(odd_ref)
    for m in range(2):
        for lev in range(2):
            for y in range(8):
                dst = even_ref if y % 2 == 0 else odd_ref
                row = ((m * 4 + y // 2) * 2 + lev) * 8
                dst[pl.ds(row, 5), :] = state_ref[pl.ds(m * 80 + lev * 8 + y, 5, stride=16), :]
                dst[pl.ds(row + 5, 1), :] = noise_ref[m, member, lev, pl.ds(y, 1), :]
                dst[pl.ds(row + 6, 1), :] = land_ref[pl.ds(y, 1), :].astype(F32)
    total = jnp.zeros((128, 128), F32)
    for ylo, ref in ((0, even_ref), (1, odd_ref)):
        x = iota((64, 128), 0)
        lane = iota((64, 128), 1)
        spread = jnp.where(lane == (x % 2) * 64 + ylo * 32 + x // 2, 1.0, 0.0).astype(BF16)
        rest = ref[...]
        for _ in range(3):
            part = rest.astype(BF16)
            total = total + nn(part, spread)
            rest = rest - part.astype(F32)
    for z in range(GROUP):
        out_ref[z] = total[(z % 2) * 64 : (z % 2) * 64 + 64]


def shift_down(v):
    keep = iota(v.shape, 0) % 32 != 0
    return jnp.where(keep, pltpu.roll(v, 1, 0), 0.0)


def shift_up(v):
    keep = iota(v.shape, 0) % 32 != 31
    return jnp.where(keep, pltpu.roll(v, v.shape[0] - 1, 0), 0.0)


def net_kernel(
    local_ref,
    rim_ref,
    embed_ref,
    merge_ref,
    expand_ref,
    head_ref,
    fine_hbm,
    coarse_hbm,
    out_ref,
    fine_w,
    coarse_w,
    ew_ref,
    f_ref,
    ee,
    eo,
    es1,
    es2,
    de,
    do,
    ds1,
    ds2,
    ca,
    cb,
    sems,
):
    space = lax.axis_index("space")
    upper = (space // 2) % 2 == 1
    first = space < 2
    last = space >= TILES - 2

    copies = [pltpu.make_async_copy(fine_hbm.at[0], fine_w.at[0], sems.at[0])]
    for k in range(4):
        copies.append(pltpu.make_async_copy(coarse_hbm.at[k], coarse_w.at[k], sems.at[1 + k]))
    copies.append(pltpu.make_async_copy(fine_hbm.at[1], fine_w.at[1], sems.at[5]))
    for copy in copies:
        copy.start()

    for j in range(20):
        low = rim_ref[pl.ds(j * 16, 16), :] if j < 6 else local_ref[pl.ds((j - 6) * 16, 16), :]
        high = (
            local_ref[pl.ds((j + 2) * 16, 16), :] if j < 14 else rim_ref[pl.ds((j - 14) * 16, 16), :]
        )
        f_ref[pl.ds(j * 16, 16), :] = jnp.where(upper, high, low)

    ew_ref[...] = jnp.zeros_like(ew_ref)
    ew_ref[pl.ds(0, 7), :] = embed_ref[...]
    w = ew_ref[...]
    w_hi = w.astype(BF16).astype(F32)
    w_lo = w - w_hi
    w4 = jnp.concatenate([w_hi, w_hi, w_lo, w_lo], axis=0).astype(BF16)

    per = 4
    def embed_block(i, _):
        for lev in range(2):
            parts = []
            for j in range(per):
                t = f_ref[pl.ds(pl.multiple_of((i * per + j) * 16 + lev * 8, 8), 8), :]
                hi = t.astype(BF16).astype(F32)
                lo = t - hi
                parts.append(jnp.concatenate([hi, lo, hi, lo], axis=0).T)
            feats = jnp.concatenate(parts, axis=0).astype(BF16)
            g = gelu(nn(feats, w4))
            even = jnp.concatenate([g[j * 128 : j * 128 + 64] for j in range(per)], axis=0)
            odd = jnp.concatenate([g[j * 128 + 64 : j * 128 + 128] for j in range(per)], axis=0)
            rows = pl.ds(pl.multiple_of(i * per * 64, 64), per * 64)
            lanes = pl.ds(lev * 256, 256)
            ee[rows, lanes] = even.astype(BF16)
            eo[rows, lanes] = odd.astype(BF16)
            es1[rows, lanes] = shift_down(odd).astype(BF16)
            es2[rows, lanes] = shift_up(even).astype(BF16)
        return 0

    lax.fori_loop(0, 20 // per, embed_block, 0)

    def fine_conv(layer, row, n, srcs):
        e, o, s1, s2 = srcs
        sides = ((s1, e), (e, o), (o, s2))
        acc = None
        for dy in range(3):
            for dx in range(3):
                rows = pl.ds((row + dy) * 32, n * 32)
                a, b = sides[dx]
                lhs = jnp.concatenate([a[rows, :], b[rows, :]], axis=0)
                taps = [
                    fine_w[layer, pl.ds(((dz * 3 + dy) * 3 + dx) * 256, 256), :] for dz in range(3)
                ]
                rhs = jnp.concatenate(
                    [
                        jnp.concatenate([taps[1], taps[0]], axis=1),
                        jnp.concatenate([taps[2], taps[1]], axis=1),
                    ],
                    axis=0,
                )
                term = nn(lhs, rhs)
                acc = term if acc is None else acc + term
        return acc

    copies[0].wait()
    for blk in range(36 // R1):
        row = blk * R1
        g = gelu(fine_conv(0, row + 1, R1, (ee, eo, es1, es2)))
        even, odd = g[: R1 * 32], g[R1 * 32 :]
        rows = pl.ds(row * 32, R1 * 32)
        odd_s, even_s = shift_down(odd), shift_up(even)
        for lev in range(2):
            src = slice(lev * 128, lev * 128 + 128)
            dst = pl.ds(lev * 256 + 128, 128)
            de[rows, dst] = even[:, src].astype(BF16)
            do[rows, dst] = odd[:, src].astype(BF16)
            ds1[rows, dst] = odd_s[:, src].astype(BF16)
            ds2[rows, dst] = even_s[:, src].astype(BF16)

    @pl.when(first)
    def _():
        for ref in (de, do, ds1, ds2):
            ref[pl.ds(0, 320), :] = jnp.zeros((320, 512), BF16)

    @pl.when(last)
    def _():
        for ref in (de, do, ds1, ds2):
            ref[pl.ds(26 * 32, 320), :] = jnp.zeros((320, 512), BF16)

    def keep_coarse(dst, lev, v):
        lanes = pl.ds(lev * 256, 256)
        rows = pl.ds(0, v.shape[0])
        dst[1, rows, lanes] = v.astype(BF16)
        dst[0, rows, lanes] = shift_down(v).astype(BF16)
        dst[2, rows, lanes] = shift_up(v).astype(BF16)

    for lev in range(2):
        lanes = pl.ds(lev * 256 + 128, 128)
        pieces = [
            jnp.concatenate([ref[pl.ds((2 * r + dy) * 32, 32), lanes] for r in range(18)], axis=0)
            for dy in range(2)
            for ref in (de, do)
        ]
        keep_coarse(ca, lev, gelu(nn(jnp.concatenate(pieces, axis=1), merge_ref[...])))

    src, dst = ca, cb
    for k in range(4):
        n = 16 - 2 * k
        copies[1 + k].wait()
        acc = [None, None]
        for dy in range(3):
            for dx in range(3):
                lhs = src[dx, pl.ds(dy * 32, n * 32), :]
                taps = [
                    coarse_w[k, pl.ds(((dz * 3 + dy) * 3 + dx) * 256, 256), :] for dz in range(3)
                ]
                for lev in range(2):
                    rhs = jnp.concatenate(
                        [taps[1], taps[2]] if lev == 0 else [taps[0], taps[1]], axis=0
                    )
                    term = nn(lhs, rhs)
                    acc[lev] = term if acc[lev] is None else acc[lev] + term
        for lev in range(2):
            before = src[1, pl.ds(32, n * 32), pl.ds(lev * 256, 256)].astype(F32)
            keep_coarse(dst, lev, before + gelu(acc[lev]))
        edge = 4 - k

        @pl.when(first)
        def _(dst=dst, edge=edge):
            dst[:, pl.ds(0, edge * 32), :] = jnp.zeros((3, edge * 32, 512), BF16)

        @pl.when(last)
        def _(dst=dst, edge=edge, n=n):
            dst[:, pl.ds((n - edge) * 32, edge * 32), :] = jnp.zeros((3, edge * 32, 512), BF16)

        src, dst = dst, src

    for lev in range(2):
        up = nn(src[1, pl.ds(0, 320), pl.ds(lev * 256, 256)], expand_ref[...])
        lanes = pl.ds(lev * 256, 128)
        down, high = shift_down(up), shift_up(up)
        for d in range(18):
            r, dy = (d + 1) // 2, (d + 1) % 2
            rows = pl.ds((d + 9) * 32, 32)
            even = slice(dy * 256, dy * 256 + 128)
            odd = slice(dy * 256 + 128, dy * 256 + 256)
            here = slice(r * 32, r * 32 + 32)
            de[rows, lanes] = up[here, even].astype(BF16)
            do[rows, lanes] = up[here, odd].astype(BF16)
            ds1[rows, lanes] = down[here, odd].astype(BF16)
            ds2[rows, lanes] = high[here, even].astype(BF16)

    row_id = iota((16, 5), 0)
    var_id = iota((16, 5), 1)
    head = jnp.concatenate(
        [
            nt(jnp.where(row_id == 2 * var_id + lev, 1.0, 0.0).astype(BF16), head_ref[...])
            for lev in range(2)
        ],
        axis=1,
    ).astype(BF16)

    src_lane = iota((512, 512), 0)
    dst_lane = iota((512, 512), 1)
    lon = 2 * (src_lane % 32) + src_lane // 256
    lat = (src_lane // 32) % 8
    spread = jnp.where(dst_lane == (lon // 16) * 128 + lat * 16 + lon % 16, 1.0, 0.0).astype(BF16)

    copies[5].wait()
    for half in range(2):
        evens, odds = [], []
        for blk in range(8 // R2):
            row = half * 8 + blk * R2
            g = gelu(fine_conv(1, row + 9, R2, (de, do, ds1, ds2))).astype(BF16)
            evens.append(g[: R2 * 32])
            odds.append(g[R2 * 32 :])
        add = nt(head, jnp.concatenate(evens + odds, axis=0))
        hi = add.astype(BF16)
        lo = (add - hi.astype(F32)).astype(BF16)
        both = nn(jnp.concatenate([hi, lo], axis=0), spread)
        both = both[:16] + both[16:]
        for s in range(SEGMENTS):
            out_ref[s * 2 + half] = both[:, s * 128 : s * 128 + 128]


def score_kernel(got_ref, state_ref, truth_ref, pred_ref, crps_ref):
    segment = lax.axis_index("segment")
    space = lax.axis_index("space")
    lane = iota((10, 128), 1)

    def block_rows(ref, start, lanes_from):
        total = jnp.zeros((10, 128), F32)
        for y in range(8):
            v = ref[pl.ds(start + y, 10, stride=8), :]
            v = jnp.concatenate([v, jnp.zeros((10, 128 - v.shape[1]), F32)], axis=1)
            v = pltpu.roll(v, lax.rem(y * 16 - lanes_from + 128, 128), 1)
            total = jnp.where(lane // 16 == y, v, total)
        return total

    def put(ref, start, v):
        for y in range(8):
            w = pltpu.roll(v, (128 - 16 * y) % 128, 1) if y else v
            ref[pl.ds(start + y, 10, stride=8), :] = w[:, :16]

    for m in range(2):
        state = block_rows(state_ref, m * 80, segment * 16)
        truth = block_rows(truth_ref, m * 80, 0)
        preds = []
        for b in range(4):
            src = member_of(b, space) * 2 + m
            preds.append(got_ref[src][:10] + state)
            put(pred_ref, (m * 4 + b) * 80, preds[b])
        skill = sum(jnp.abs(p - truth) for p in preds) * 0.25
        spread = sum(
            jnp.abs(preds[b] - preds[c]) for b in range(4) for c in range(b + 1, 4)
        )
        put(crps_ref, m * 80, skill - spread * (1.0 / 12.0))


def index(segment, column, z):
    return segment * TILES + column * GROUP + z


def body(
    state,
    noise,
    land_sea,
    observed_truth,
    embed_w,
    fine_weight_kernels,
    merge_w,
    coarse_w,
    expand_w,
    head_w,
):
    space = lax.axis_index("space")
    columns = TILES // GROUP
    state_rows = state.reshape(160, 64)
    params = pltpu.CompilerParams(vmem_limit_bytes=VMEM_LIMIT)
    vmem = pl.BlockSpec(memory_space=pltpu.VMEM)
    hbm = pl.BlockSpec(memory_space=pl.ANY)

    packed = pl.pallas_call(
        pack_kernel,
        out_shape=jax.ShapeDtypeStruct((GROUP, 64, 128), F32),
        in_specs=[vmem] * 3,
        out_specs=vmem,
        scratch_shapes=[pltpu.VMEM((128, 64), F32), pltpu.VMEM((128, 64), F32)],
        name="pack",
    )(state_rows, noise, land_sea)

    rings = [
        [index(s, c, z) for z in range(GROUP)] for s in range(SEGMENTS) for c in range(columns)
    ]
    local = lax.all_to_all(packed, AXES, 0, 0, axis_index_groups=rings, tiled=True)
    local = local.reshape(256, 128)

    pairs = []
    for s in range(SEGMENTS):
        for c in range(1, columns):
            for z in range(2):
                here, there = index(s, c, z), index(s ^ 2, c - 1, z + 2)
                pairs += [(here, there), (there, here)]
    upper = (space // 2) % 2
    rim = lax.ppermute(jnp.where(upper == 1, local[160:256], local[0:96]), AXES, pairs)

    e_buf = pltpu.VMEM((40 * 32, 512), BF16)
    d_buf = pltpu.VMEM((36 * 32, 512), BF16)
    increments = pl.pallas_call(
        net_kernel,
        out_shape=jax.ShapeDtypeStruct((8, 16, 128), F32),
        in_specs=[vmem] * 6 + [hbm] * 2,
        out_specs=vmem,
        scratch_shapes=[
            pltpu.VMEM((2, 6912, 128), BF16),
            pltpu.VMEM((4, 6912, 256), BF16),
            pltpu.VMEM((8, 256), F32),
            pltpu.VMEM((320, 128), F32),
            *[e_buf] * 4,
            *[d_buf] * 4,
            pltpu.VMEM((3, 576, 512), BF16),
            pltpu.VMEM((3, 576, 512), BF16),
            pltpu.SemaphoreType.DMA((6,)),
        ],
        compiler_params=params,
        name="net",
    )(local, rim, embed_w, merge_w, expand_w, head_w, fine_weight_kernels, coarse_w)

    squares = [
        [index(s, c, 2 * h + r) for s in range(SEGMENTS) for r in range(2)]
        for c in range(columns)
        for h in range(2)
    ]
    got = lax.all_to_all(increments, AXES, 0, 0, axis_index_groups=squares, tiled=True)

    prediction, crps = pl.pallas_call(
        score_kernel,
        out_shape=(
            jax.ShapeDtypeStruct((640, 16), F32),
            jax.ShapeDtypeStruct((160, 16), F32),
        ),
        in_specs=[vmem] * 3,
        out_specs=(vmem, vmem),
        name="score",
    )(got, state_rows, observed_truth.reshape(160, 16))
    return prediction.reshape(2, 4, 5, 2, 8, 16), crps.reshape(2, 5, 2, 8, 16)


def solution(mesh):
    return jax.shard_map(
        body,
        mesh=mesh,
        in_specs=(
            P(None, None, None, "space", None),
            P(None, None, None, "space", None),
            P("space", None),
            P(None, None, None, "space", "segment"),
            P(),
            P(),
            P(),
            P(),
            P(),
            P(),
        ),
        out_specs=(
            P(None, None, None, None, "space", "segment"),
            P(None, None, None, "space", "segment"),
        ),
        check_vma=False,
    )
```

```python
import jax
import jax.numpy as jnp
from jax import lax
from jax.experimental import pallas as pl
from jax.experimental.pallas import tpu as pltpu
from jax.sharding import PartitionSpec as P

F32 = jnp.float32
BF16 = jnp.bfloat16
AXES = ("segment", "space")
SEGMENTS = 4
TILES = 32
GROUP = 4
VMEM_LIMIT = 50 * 1024 * 1024
SMALL_LIMIT = 8 * 1024 * 1024
R1 = 6
RC = 1
R2 = 4


def gelu(x):
    half = 0.5 * x
    t = jnp.tanh(x * (0.7978845608028654 + 0.035677408136300125 * (x * x)))
    return half + half * t


def nn(a, b):
    return lax.dot_general(a, b, (((1,), (0,)), ((), ())), preferred_element_type=F32)


def nt(a, b):
    return lax.dot_general(a, b, (((1,), (1,)), ((), ())), preferred_element_type=F32)


def iota(shape, dim):
    return lax.broadcasted_iota(jnp.int32, shape, dim)


def member_of(segment, space):
    return segment ^ (2 * ((space // GROUP) % 2))


def pack_kernel(state_ref, noise_ref, land_ref, own_ref, other_ref, even_ref, odd_ref):
    member = member_of(lax.axis_index("segment"), lax.axis_index("space"))
    even_ref[...] = jnp.zeros_like(even_ref)
    odd_ref[...] = jnp.zeros_like(odd_ref)
    for m in range(2):
        for lev in range(2):
            for y in range(8):
                dst = even_ref if y % 2 == 0 else odd_ref
                row = ((m * 4 + y // 2) * 2 + lev) * 8
                dst[pl.ds(row, 5), :] = state_ref[pl.ds(m * 80 + lev * 8 + y, 5, stride=16), :]
                dst[pl.ds(row + 5, 1), :] = noise_ref[m, member, lev, pl.ds(y, 1), :]
                dst[pl.ds(row + 6, 1), :] = land_ref[pl.ds(y, 1), :].astype(F32)
    total = jnp.zeros((128, 128), F32)
    for ylo, ref in ((0, even_ref), (1, odd_ref)):
        x = iota((64, 128), 0)
        lane = iota((64, 128), 1)
        spread = jnp.where(lane == (x % 2) * 64 + ylo * 32 + x // 2, 1.0, 0.0).astype(BF16)
        rest = ref[...]
        for _ in range(3):
            part = rest.astype(BF16)
            total = total + nn(part, spread)
            rest = rest - part.astype(F32)
    odd = lax.axis_index("space") % 2 == 1
    own_ref[...] = jnp.where(odd, total[64:], total[:64])
    other_ref[...] = jnp.where(odd, total[:64], total[64:])


def join_kernel(own_ref, got_ref, pair_ref, near_ref, far_ref):
    space = lax.axis_index("space")
    odd = space % 2 == 1
    upper = (space // 2) % 2 == 1
    pair_ref[pl.ds(0, 64), :] = jnp.where(odd, got_ref[...], own_ref[...])
    pair_ref[pl.ds(64, 64), :] = jnp.where(odd, own_ref[...], got_ref[...])
    head, tail = pair_ref[pl.ds(0, 96), :], pair_ref[pl.ds(32, 96), :]
    near_ref[...] = jnp.where(upper, head, tail)
    far_ref[...] = jnp.where(upper, tail, head)


def shift_down(v):
    keep = iota(v.shape, 0) % 32 != 0
    return jnp.where(keep, pltpu.roll(v, 1, 0), 0.0)


def shift_up(v):
    keep = iota(v.shape, 0) % 32 != 31
    return jnp.where(keep, pltpu.roll(v, v.shape[0] - 1, 0), 0.0)


def net_kernel(
    pair_ref,
    near_ref,
    far_ref,
    embed_ref,
    merge_ref,
    expand_ref,
    head_ref,
    fine_hbm,
    coarse_hbm,
    out_ref,
    fine_w,
    coarse_w,
    ew_ref,
    f_ref,
    ee,
    eo,
    es1,
    es2,
    de,
    do,
    ds1,
    ds2,
    ca,
    cb,
    sems,
):
    space = lax.axis_index("space")
    upper = (space // 2) % 2 == 1
    first = space < 2
    last = space >= TILES - 2

    copies = [pltpu.make_async_copy(fine_hbm.at[0], fine_w.at[0], sems.at[0])]
    for k in range(4):
        copies.append(pltpu.make_async_copy(coarse_hbm.at[k], coarse_w.at[k], sems.at[1 + k]))
    copies.append(pltpu.make_async_copy(fine_hbm.at[1], fine_w.at[1], sems.at[5]))
    for copy in copies:
        copy.start()

    near, far = near_ref[...], far_ref[...]
    f_ref[pl.ds(0, 96), :] = jnp.where(upper, near, far)
    f_ref[pl.ds(96, 128), :] = pair_ref[...]
    f_ref[pl.ds(224, 96), :] = jnp.where(upper, far, near)

    ew_ref[...] = jnp.zeros_like(ew_ref)
    ew_ref[pl.ds(0, 7), :] = embed_ref[...]
    w = ew_ref[...]
    w_hi = w.astype(BF16).astype(F32)
    w_lo = w - w_hi
    w4 = jnp.concatenate([w_hi, w_hi, w_lo, w_lo], axis=0).astype(BF16)

    per = 4
    def embed_block(i, _):
        for lev in range(2):
            parts = []
            for j in range(per):
                t = f_ref[pl.ds(pl.multiple_of((i * per + j) * 16 + lev * 8, 8), 8), :]
                hi = t.astype(BF16).astype(F32)
                lo = t - hi
                parts.append(jnp.concatenate([hi, lo, hi, lo], axis=0).T)
            feats = jnp.concatenate(parts, axis=0).astype(BF16)
            g = gelu(nn(feats, w4))
            even = jnp.concatenate([g[j * 128 : j * 128 + 64] for j in range(per)], axis=0)
            odd = jnp.concatenate([g[j * 128 + 64 : j * 128 + 128] for j in range(per)], axis=0)
            rows = pl.ds(pl.multiple_of(i * per * 64, 64), per * 64)
            lanes = pl.ds(lev * 256, 256)
            ee[rows, lanes] = even.astype(BF16)
            eo[rows, lanes] = odd.astype(BF16)
            es1[rows, lanes] = shift_down(odd).astype(BF16)
            es2[rows, lanes] = shift_up(even).astype(BF16)
        return 0

    lax.fori_loop(0, 20 // per, embed_block, 0)

    def fine_conv(layer, row, n, srcs):
        e, o, s1, s2 = srcs
        sides = ((s1, e), (e, o), (o, s2))
        acc = None
        for dy in range(3):
            for dx in range(3):
                rows = pl.ds((row + dy) * 32, n * 32)
                a, b = sides[dx]
                lhs = jnp.concatenate([a[rows, :], b[rows, :]], axis=0)
                taps = [
                    fine_w[layer, pl.ds(((dz * 3 + dy) * 3 + dx) * 256, 256), :] for dz in range(3)
                ]
                rhs = jnp.concatenate(
                    [
                        jnp.concatenate([taps[1], taps[0]], axis=1),
                        jnp.concatenate([taps[2], taps[1]], axis=1),
                    ],
                    axis=0,
                )
                term = nn(lhs, rhs)
                acc = term if acc is None else acc + term
        return acc

    copies[0].wait()
    for blk in range(36 // R1):
        row = blk * R1
        g = gelu(fine_conv(0, row + 1, R1, (ee, eo, es1, es2)))
        even, odd = g[: R1 * 32], g[R1 * 32 :]
        rows = pl.ds(row * 32, R1 * 32)
        odd_s, even_s = shift_down(odd), shift_up(even)
        for lev in range(2):
            src = slice(lev * 128, lev * 128 + 128)
            dst = pl.ds(lev * 256 + 128, 128)
            de[rows, dst] = even[:, src].astype(BF16)
            do[rows, dst] = odd[:, src].astype(BF16)
            ds1[rows, dst] = odd_s[:, src].astype(BF16)
            ds2[rows, dst] = even_s[:, src].astype(BF16)

    @pl.when(first)
    def _():
        for ref in (de, do, ds1, ds2):
            ref[pl.ds(0, 320), :] = jnp.zeros((320, 512), BF16)

    @pl.when(last)
    def _():
        for ref in (de, do, ds1, ds2):
            ref[pl.ds(26 * 32, 320), :] = jnp.zeros((320, 512), BF16)

    def keep_coarse(dst, lev, v, start):
        lanes = pl.ds(lev * 256, 256)
        rows = pl.ds(start, v.shape[0])
        dst[1, rows, lanes] = v.astype(BF16)
        dst[0, rows, lanes] = shift_down(v).astype(BF16)
        dst[2, rows, lanes] = shift_up(v).astype(BF16)

    for lev in range(2):
        lanes = pl.ds(lev * 256 + 128, 128)
        pieces = [
            jnp.concatenate([ref[pl.ds((2 * r + dy) * 32, 32), lanes] for r in range(18)], axis=0)
            for dy in range(2)
            for ref in (de, do)
        ]
        keep_coarse(ca, lev, gelu(nn(jnp.concatenate(pieces, axis=1), merge_ref[...])), 0)

    src, dst = ca, cb
    for k in range(4):
        n = 16 - 2 * k
        copies[1 + k].wait()
        blocks = range(0, n, n // RC)
        for row in blocks:
            size = n // RC
            acc = [None, None]
            for dy in range(3):
                for dx in range(3):
                    lhs = src[dx, pl.ds((row + dy) * 32, size * 32), :]
                    taps = [
                        coarse_w[k, pl.ds(((dz * 3 + dy) * 3 + dx) * 256, 256), :]
                        for dz in range(3)
                    ]
                    for lev in range(2):
                        rhs = jnp.concatenate(
                            [taps[1], taps[2]] if lev == 0 else [taps[0], taps[1]], axis=0
                        )
                        term = nn(lhs, rhs)
                        acc[lev] = term if acc[lev] is None else acc[lev] + term
            for lev in range(2):
                before = src[1, pl.ds((row + 1) * 32, size * 32), pl.ds(lev * 256, 256)]
                keep_coarse(dst, lev, before.astype(F32) + gelu(acc[lev]), row * 32)
        edge = 4 - k

        @pl.when(first)
        def _(dst=dst, edge=edge):
            dst[:, pl.ds(0, edge * 32), :] = jnp.zeros((3, edge * 32, 512), BF16)

        @pl.when(last)
        def _(dst=dst, edge=edge, n=n):
            dst[:, pl.ds((n - edge) * 32, edge * 32), :] = jnp.zeros((3, edge * 32, 512), BF16)

        src, dst = dst, src

    for lev in range(2):
        up = nn(src[1, pl.ds(0, 320), pl.ds(lev * 256, 256)], expand_ref[...])
        lanes = pl.ds(lev * 256, 128)
        down, high = shift_down(up), shift_up(up)
        for d in range(18):
            r, dy = (d + 1) // 2, (d + 1) % 2
            rows = pl.ds((d + 9) * 32, 32)
            even = slice(dy * 256, dy * 256 + 128)
            odd = slice(dy * 256 + 128, dy * 256 + 256)
            here = slice(r * 32, r * 32 + 32)
            de[rows, lanes] = up[here, even].astype(BF16)
            do[rows, lanes] = up[here, odd].astype(BF16)
            ds1[rows, lanes] = down[here, odd].astype(BF16)
            ds2[rows, lanes] = high[here, even].astype(BF16)

    row_id = iota((16, 5), 0)
    var_id = iota((16, 5), 1)
    head = jnp.concatenate(
        [
            nn(jnp.where(row_id == 2 * var_id + lev, 1.0, 0.0).astype(BF16), head_ref[...])
            for lev in range(2)
        ],
        axis=1,
    ).astype(BF16)

    src_lane = iota((512, 512), 0)
    dst_lane = iota((512, 512), 1)
    lon = 2 * (src_lane % 32) + src_lane // 256
    lat = (src_lane // 32) % 8
    spread = jnp.where(dst_lane == (lon // 16) * 128 + lat * 16 + lon % 16, 1.0, 0.0).astype(BF16)

    copies[5].wait()
    for half in range(2):
        evens, odds = [], []
        for blk in range(8 // R2):
            row = half * 8 + blk * R2
            g = gelu(fine_conv(1, row + 9, R2, (de, do, ds1, ds2))).astype(BF16)
            evens.append(g[: R2 * 32])
            odds.append(g[R2 * 32 :])
        add = nt(head, jnp.concatenate(evens + odds, axis=0))
        hi = add.astype(BF16)
        lo = (add - hi.astype(F32)).astype(BF16)
        both = nn(jnp.concatenate([hi, lo], axis=0), spread)
        both = both[:16] + both[16:]
        for s in range(SEGMENTS):
            out_ref[s * 2 + half] = both[:, s * 128 : s * 128 + 128]


def score_kernel(got_ref, state_ref, truth_ref, pred_ref, crps_ref):
    segment = lax.axis_index("segment")
    space = lax.axis_index("space")
    lane = iota((10, 128), 1)

    def block_rows(ref, start, lanes_from):
        total = jnp.zeros((10, 128), F32)
        for y in range(8):
            v = ref[pl.ds(start + y, 10, stride=8), :]
            v = jnp.concatenate([v, jnp.zeros((10, 128 - v.shape[1]), F32)], axis=1)
            v = pltpu.roll(v, lax.rem(y * 16 - lanes_from + 128, 128), 1)
            total = jnp.where(lane // 16 == y, v, total)
        return total

    def put(ref, start, v):
        for y in range(8):
            w = pltpu.roll(v, (128 - 16 * y) % 128, 1) if y else v
            ref[pl.ds(start + y, 10, stride=8), :] = w[:, :16]

    for m in range(2):
        state = block_rows(state_ref, m * 80, segment * 16)
        truth = block_rows(truth_ref, m * 80, 0)
        preds = []
        for b in range(4):
            src = member_of(b, space) * 2 + m
            preds.append(got_ref[src][:10] + state)
            put(pred_ref, (m * 4 + b) * 80, preds[b])
        skill = sum(jnp.abs(p - truth) for p in preds) * 0.25
        spread = sum(
            jnp.abs(preds[b] - preds[c]) for b in range(4) for c in range(b + 1, 4)
        )
        put(crps_ref, m * 80, skill - spread * (1.0 / 12.0))


def run_net(pair, near, far, embed_w, merge_w, expand_w, head_w, fine_weight_kernels, coarse_w):
    params = pltpu.CompilerParams(vmem_limit_bytes=VMEM_LIMIT)
    vmem = pl.BlockSpec(memory_space=pltpu.VMEM)
    hbm = pl.BlockSpec(memory_space=pl.ANY)
    e_buf = pltpu.VMEM((40 * 32, 512), BF16)
    d_buf = pltpu.VMEM((36 * 32, 512), BF16)
    increments = pl.pallas_call(
        net_kernel,
        out_shape=jax.ShapeDtypeStruct((8, 16, 128), F32),
        in_specs=[vmem] * 7 + [hbm] * 2,
        out_specs=vmem,
        scratch_shapes=[
            pltpu.VMEM((2, 6912, 128), BF16),
            pltpu.VMEM((4, 6912, 256), BF16),
            pltpu.VMEM((8, 256), F32),
            pltpu.VMEM((320, 128), F32),
            *[e_buf] * 4,
            *[d_buf] * 4,
            pltpu.VMEM((3, 576, 512), BF16),
            pltpu.VMEM((3, 576, 512), BF16),
            pltpu.SemaphoreType.DMA((6,)),
        ],
        compiler_params=params,
        name="net",
    )(pair, near, far, embed_w, merge_w, expand_w, head_w, fine_weight_kernels, coarse_w)
    return increments


def index(segment, column, z):
    return segment * TILES + column * GROUP + z


def body(
    state,
    noise,
    land_sea,
    observed_truth,
    embed_w,
    fine_weight_kernels,
    merge_w,
    coarse_w,
    expand_w,
    head_w,
):
    columns = TILES // GROUP
    state_rows = state.reshape(160, 64)
    vmem = pl.BlockSpec(memory_space=pltpu.VMEM)

    small = pltpu.CompilerParams(vmem_limit_bytes=SMALL_LIMIT)
    tile = jax.ShapeDtypeStruct((64, 128), F32)
    own, other = pl.pallas_call(
        pack_kernel,
        out_shape=(tile, tile),
        in_specs=[vmem] * 3,
        out_specs=(vmem, vmem),
        scratch_shapes=[pltpu.VMEM((128, 64), F32), pltpu.VMEM((128, 64), F32)],
        compiler_params=small,
        name="pack",
    )(state_rows, noise, land_sea)

    every = [(s, c, z) for s in range(SEGMENTS) for c in range(columns) for z in range(GROUP)]
    beside = [(index(s, c, z), index(s, c, z ^ 1)) for s, c, z in every]
    across = [(index(s, c, z), index(s, c, z ^ 2)) for s, c, z in every]
    beyond = []
    for s, c, z in every:
        if c > 0 and z < 2:
            here, there = index(s, c, z), index(s ^ 2, c - 1, z + 2)
            beyond += [(here, there), (there, here)]

    got = lax.ppermute(other, AXES, beside)
    rows12 = jax.ShapeDtypeStruct((96, 128), F32)
    pair, near, far = pl.pallas_call(
        join_kernel,
        out_shape=(jax.ShapeDtypeStruct((128, 128), F32), rows12, rows12),
        in_specs=[vmem] * 2,
        out_specs=(vmem,) * 3,
        compiler_params=small,
        name="join",
    )(own, got)
    far = lax.ppermute(far, AXES, beyond)
    near = lax.ppermute(near, AXES, across)
    increments = run_net(
        pair, near, far, embed_w, merge_w, expand_w, head_w.T, fine_weight_kernels, coarse_w
    )

    squares = [
        [index(s, c, 2 * h + r) for s in range(SEGMENTS) for r in range(2)]
        for c in range(columns)
        for h in range(2)
    ]
    got = lax.all_to_all(increments, AXES, 0, 0, axis_index_groups=squares, tiled=True)

    prediction, crps = pl.pallas_call(
        score_kernel,
        out_shape=(
            jax.ShapeDtypeStruct((640, 16), F32),
            jax.ShapeDtypeStruct((160, 16), F32),
        ),
        in_specs=[vmem] * 3,
        out_specs=(vmem, vmem),
        compiler_params=small,
        name="score",
    )(got, state_rows, observed_truth.reshape(160, 16))
    return prediction.reshape(2, 4, 5, 2, 8, 16), crps.reshape(2, 5, 2, 8, 16)


def solution(mesh):
    return jax.shard_map(
        body,
        mesh=mesh,
        in_specs=(
            P(None, None, None, "space", None),
            P(None, None, None, "space", None),
            P("space", None),
            P(None, None, None, "space", "segment"),
            P(),
            P(),
            P(),
            P(),
            P(),
            P(),
        ),
        out_specs=(
            P(None, None, None, None, "space", "segment"),
            P(None, None, None, "space", "segment"),
        ),
        check_vma=False,
    )
```

```python
import jax
import jax.numpy as jnp
from jax import lax
from jax.experimental import pallas as pl
from jax.experimental.pallas import tpu as pltpu
from jax.sharding import PartitionSpec as P

F32 = jnp.float32
BF16 = jnp.bfloat16
AXES = ("segment", "space")
SEGMENTS = 4
TILES = 32
GROUP = 4
VMEM_LIMIT = 50 * 1024 * 1024
SMALL_LIMIT = 8 * 1024 * 1024
R1 = 9
RC = 1
R2 = 4


def gelu(x):
    half = 0.5 * x
    t = jnp.tanh(x * (0.7978845608028654 + 0.035677408136300125 * (x * x)))
    return half + half * t


def nn(a, b):
    return lax.dot_general(a, b, (((1,), (0,)), ((), ())), preferred_element_type=F32)


def nt(a, b):
    return lax.dot_general(a, b, (((1,), (1,)), ((), ())), preferred_element_type=F32)


def iota(shape, dim):
    return lax.broadcasted_iota(jnp.int32, shape, dim)


def member_of(segment, space):
    return segment ^ (2 * ((space // GROUP) % 2))


def pack_kernel(
    state_hbm,
    noise_hbm,
    land_hbm,
    own_ref,
    other_ref,
    state_ref,
    noise_ref,
    land_ref,
    even_ref,
    odd_ref,
    sems,
):
    member = member_of(lax.axis_index("segment"), lax.axis_index("space"))
    copies = [
        pltpu.make_async_copy(state_hbm, state_ref, sems.at[0]),
        pltpu.make_async_copy(noise_hbm, noise_ref, sems.at[1]),
        pltpu.make_async_copy(land_hbm, land_ref, sems.at[2]),
    ]
    for copy in copies:
        copy.start()
    even_ref[...] = jnp.zeros_like(even_ref)
    odd_ref[...] = jnp.zeros_like(odd_ref)
    for copy in copies:
        copy.wait()
    for m in range(2):
        for lev in range(2):
            for y in range(8):
                dst = even_ref if y % 2 == 0 else odd_ref
                row = ((m * 4 + y // 2) * 2 + lev) * 8
                dst[pl.ds(row, 5), :] = state_ref[pl.ds(m * 80 + lev * 8 + y, 5, stride=16), :]
                dst[pl.ds(row + 5, 1), :] = noise_ref[m, member, lev, pl.ds(y, 1), :]
                dst[pl.ds(row + 6, 1), :] = land_ref[pl.ds(y, 1), :].astype(F32)
    total = jnp.zeros((128, 128), F32)
    for ylo, ref in ((0, even_ref), (1, odd_ref)):
        x = iota((64, 128), 0)
        lane = iota((64, 128), 1)
        spread = jnp.where(lane == (x % 2) * 64 + ylo * 32 + x // 2, 1.0, 0.0).astype(BF16)
        rest = ref[...]
        for _ in range(3):
            part = rest.astype(BF16)
            total = total + nn(part, spread)
            rest = rest - part.astype(F32)
    odd = lax.axis_index("space") % 2 == 1
    own_ref[...] = jnp.where(odd, total[64:], total[:64])
    other_ref[...] = jnp.where(odd, total[:64], total[64:])


def join_kernel(own_ref, got_ref, pair_ref, near_ref, far_ref):
    space = lax.axis_index("space")
    odd = space % 2 == 1
    upper = (space // 2) % 2 == 1
    pair_ref[pl.ds(0, 64), :] = jnp.where(odd, got_ref[...], own_ref[...])
    pair_ref[pl.ds(64, 64), :] = jnp.where(odd, own_ref[...], got_ref[...])
    head, tail = pair_ref[pl.ds(0, 96), :], pair_ref[pl.ds(32, 96), :]
    near_ref[...] = jnp.where(upper, head, tail)
    far_ref[...] = jnp.where(upper, tail, head)


def run_mask(v, row):
    runs = v.reshape(v.shape[0] // 32, 32, v.shape[1])
    return jnp.where(iota((1, 32, v.shape[1]), 1) != row, runs, 0.0).reshape(v.shape)


def shift_down(v):
    return run_mask(pltpu.roll(v, 1, 0), 0)


def shift_up(v):
    return run_mask(pltpu.roll(v, v.shape[0] - 1, 0), 31)


def net_kernel(
    pair_ref,
    near_ref,
    far_ref,
    embed_hbm,
    merge_hbm,
    expand_hbm,
    head_hbm,
    fine_hbm,
    coarse_hbm,
    out_ref,
    fine_w,
    coarse_w,
    embed_ref,
    merge_ref,
    expand_ref,
    head_ref,
    ew_ref,
    f_ref,
    ee,
    eo,
    es1,
    es2,
    de,
    do,
    ds1,
    ds2,
    ca,
    cb,
    sems,
):
    space = lax.axis_index("space")
    upper = (space // 2) % 2 == 1
    first = space < 2
    last = space >= TILES - 2

    copies = [pltpu.make_async_copy(fine_hbm.at[0], fine_w.at[0], sems.at[0])]
    for k in range(4):
        copies.append(pltpu.make_async_copy(coarse_hbm.at[k], coarse_w.at[k], sems.at[1 + k]))
    copies.append(pltpu.make_async_copy(fine_hbm.at[1], fine_w.at[1], sems.at[5]))
    merge_copy = pltpu.make_async_copy(merge_hbm, merge_ref, sems.at[6])
    expand_copy = pltpu.make_async_copy(expand_hbm, expand_ref, sems.at[7])
    head_copy = pltpu.make_async_copy(head_hbm, head_ref, sems.at[8])
    embed_copy = pltpu.make_async_copy(embed_hbm, embed_ref, sems.at[9])
    for copy in (embed_copy, copies[0], merge_copy, *copies[1:], expand_copy, head_copy):
        copy.start()

    near, far = near_ref[...], far_ref[...]
    f_ref[pl.ds(0, 96), :] = jnp.where(upper, near, far)
    f_ref[pl.ds(96, 128), :] = pair_ref[...]
    f_ref[pl.ds(224, 96), :] = jnp.where(upper, far, near)

    embed_copy.wait()
    ew_ref[...] = jnp.zeros_like(ew_ref)
    ew_ref[pl.ds(0, 7), :] = embed_ref[...]
    w = ew_ref[...]
    w_hi = w.astype(BF16).astype(F32)
    w_lo = w - w_hi
    w4 = jnp.concatenate([w_hi, w_hi, w_lo, w_lo], axis=0).astype(BF16)

    per = 10
    def embed_block(i, _):
        for lev in range(2):
            parts = []
            for j in range(per):
                t = f_ref[pl.ds(pl.multiple_of((i * per + j) * 16 + lev * 8, 8), 8), :]
                hi = t.astype(BF16).astype(F32)
                lo = t - hi
                parts.append(jnp.concatenate([hi, lo, hi, lo], axis=0).T)
            feats = jnp.concatenate(parts, axis=0).astype(BF16)
            g = gelu(nn(feats, w4))
            even = jnp.concatenate([g[j * 128 : j * 128 + 64] for j in range(per)], axis=0)
            odd = jnp.concatenate([g[j * 128 + 64 : j * 128 + 128] for j in range(per)], axis=0)
            rows = pl.ds(pl.multiple_of(i * per * 64, 64), per * 64)
            lanes = pl.ds(lev * 256, 256)
            ee[rows, lanes] = even.astype(BF16)
            eo[rows, lanes] = odd.astype(BF16)
            es1[rows, lanes] = shift_down(odd).astype(BF16)
            es2[rows, lanes] = shift_up(even).astype(BF16)
        return 0

    lax.fori_loop(0, 20 // per, embed_block, 0)

    def fine_conv(layer, row, n, srcs):
        e, o, s1, s2 = srcs
        sides = ((s1, e), (e, o), (o, s2))
        acc = None
        for dy in range(3):
            for dx in range(3):
                rows = pl.ds((row + dy) * 32, n * 32)
                a, b = sides[dx]
                lhs = jnp.concatenate([a[rows, :], b[rows, :]], axis=0)
                taps = [
                    fine_w[layer, pl.ds(((dz * 3 + dy) * 3 + dx) * 256, 256), :] for dz in range(3)
                ]
                rhs = jnp.concatenate(
                    [
                        jnp.concatenate([taps[1], taps[0]], axis=1),
                        jnp.concatenate([taps[2], taps[1]], axis=1),
                    ],
                    axis=0,
                )
                term = nn(lhs, rhs)
                acc = term if acc is None else acc + term
        return acc

    copies[0].wait()
    for blk in range(36 // R1):
        row = blk * R1
        g = gelu(fine_conv(0, row + 1, R1, (ee, eo, es1, es2)))
        even, odd = g[: R1 * 32], g[R1 * 32 :]
        rows = pl.ds(row * 32, R1 * 32)
        odd_s, even_s = shift_down(odd), shift_up(even)
        for lev in range(2):
            src = slice(lev * 128, lev * 128 + 128)
            dst = pl.ds(lev * 256 + 128, 128)
            de[rows, dst] = even[:, src].astype(BF16)
            do[rows, dst] = odd[:, src].astype(BF16)
            ds1[rows, dst] = odd_s[:, src].astype(BF16)
            ds2[rows, dst] = even_s[:, src].astype(BF16)

    @pl.when(first)
    def _():
        for ref in (de, do, ds1, ds2):
            ref[pl.ds(0, 320), :] = jnp.zeros((320, 512), BF16)

    @pl.when(last)
    def _():
        for ref in (de, do, ds1, ds2):
            ref[pl.ds(26 * 32, 320), :] = jnp.zeros((320, 512), BF16)

    def keep_coarse(dst, lev, v, start):
        lanes = pl.ds(lev * 256, 256)
        rows = pl.ds(start, v.shape[0])
        dst[1, rows, lanes] = v.astype(BF16)
        dst[0, rows, lanes] = shift_down(v).astype(BF16)
        dst[2, rows, lanes] = shift_up(v).astype(BF16)

    merge_copy.wait()
    for lev in range(2):
        lanes = pl.ds(lev * 256 + 128, 128)
        pieces = [
            jnp.concatenate([ref[pl.ds((2 * r + dy) * 32, 32), lanes] for r in range(18)], axis=0)
            for dy in range(2)
            for ref in (de, do)
        ]
        keep_coarse(ca, lev, gelu(nn(jnp.concatenate(pieces, axis=1), merge_ref[...])), 0)

    src, dst = ca, cb
    for k in range(4):
        n = 16 - 2 * k
        copies[1 + k].wait()
        blocks = range(0, n, n // RC)
        for row in blocks:
            size = n // RC
            acc = [None, None]
            for dy in range(3):
                for dx in range(3):
                    lhs = src[dx, pl.ds((row + dy) * 32, size * 32), :]
                    taps = [
                        coarse_w[k, pl.ds(((dz * 3 + dy) * 3 + dx) * 256, 256), :]
                        for dz in range(3)
                    ]
                    for lev in range(2):
                        rhs = jnp.concatenate(
                            [taps[1], taps[2]] if lev == 0 else [taps[0], taps[1]], axis=0
                        )
                        term = nn(lhs, rhs)
                        acc[lev] = term if acc[lev] is None else acc[lev] + term
            for lev in range(2):
                before = src[1, pl.ds((row + 1) * 32, size * 32), pl.ds(lev * 256, 256)]
                keep_coarse(dst, lev, before.astype(F32) + gelu(acc[lev]), row * 32)
        edge = 4 - k

        @pl.when(first)
        def _(dst=dst, edge=edge):
            dst[:, pl.ds(0, edge * 32), :] = jnp.zeros((3, edge * 32, 512), BF16)

        @pl.when(last)
        def _(dst=dst, edge=edge, n=n):
            dst[:, pl.ds((n - edge) * 32, edge * 32), :] = jnp.zeros((3, edge * 32, 512), BF16)

        src, dst = dst, src

    expand_copy.wait()
    for lev in range(2):
        up = nn(src[1, pl.ds(0, 320), pl.ds(lev * 256, 256)], expand_ref[...])
        lanes = pl.ds(lev * 256, 128)
        down, high = shift_down(up), shift_up(up)
        for d in range(18):
            r, dy = (d + 1) // 2, (d + 1) % 2
            rows = pl.ds((d + 9) * 32, 32)
            even = slice(dy * 256, dy * 256 + 128)
            odd = slice(dy * 256 + 128, dy * 256 + 256)
            here = slice(r * 32, r * 32 + 32)
            de[rows, lanes] = up[here, even].astype(BF16)
            do[rows, lanes] = up[here, odd].astype(BF16)
            ds1[rows, lanes] = down[here, odd].astype(BF16)
            ds2[rows, lanes] = high[here, even].astype(BF16)

    head_copy.wait()
    row_id = iota((16, 5), 0)
    var_id = iota((16, 5), 1)
    head = jnp.concatenate(
        [
            nn(jnp.where(row_id == 2 * var_id + lev, 1.0, 0.0).astype(BF16), head_ref[...])
            for lev in range(2)
        ],
        axis=1,
    ).astype(BF16)

    src_lane = iota((512, 1), 0)
    dst_lane = iota((512, 512), 1)
    lon = 2 * (src_lane & 31) + (src_lane >> 8)
    lat = (src_lane >> 5) & 7
    place = ((lon >> 4) << 7) + (lat << 4) + (lon & 15)
    spread = jnp.where(dst_lane == place, 1.0, 0.0).astype(BF16)

    copies[5].wait()
    for half in range(2):
        evens, odds = [], []
        for blk in range(8 // R2):
            row = half * 8 + blk * R2
            g = gelu(fine_conv(1, row + 9, R2, (de, do, ds1, ds2))).astype(BF16)
            evens.append(g[: R2 * 32])
            odds.append(g[R2 * 32 :])
        add = nt(head, jnp.concatenate(evens + odds, axis=0))
        hi = add.astype(BF16)
        lo = (add - hi.astype(F32)).astype(BF16)
        both = nn(jnp.concatenate([hi, lo], axis=0), spread)
        both = both[:16] + both[16:]
        for s in range(SEGMENTS):
            out_ref[s * 2 + half] = both[:, s * 128 : s * 128 + 128]


def score_kernel(got_ref, state_ref, truth_ref, pred_ref, crps_ref):
    segment = lax.axis_index("segment")
    space = lax.axis_index("space")
    lane = iota((10, 128), 1)

    def block_rows(ref, start, lanes_from):
        total = jnp.zeros((10, 128), F32)
        for y in range(8):
            v = ref[pl.ds(start + y, 10, stride=8), :]
            v = jnp.concatenate([v, jnp.zeros((10, 128 - v.shape[1]), F32)], axis=1)
            v = pltpu.roll(v, lax.rem(y * 16 - lanes_from + 128, 128), 1)
            total = jnp.where(lane // 16 == y, v, total)
        return total

    def put(ref, start, v):
        for y in range(8):
            w = pltpu.roll(v, (128 - 16 * y) % 128, 1) if y else v
            ref[pl.ds(start + y, 10, stride=8), :] = w[:, :16]

    for m in range(2):
        state = block_rows(state_ref, m * 80, segment * 16)
        truth = block_rows(truth_ref, m * 80, 0)
        preds = []
        for b in range(4):
            src = member_of(b, space) * 2 + m
            preds.append(got_ref[src][:10] + state)
            put(pred_ref, (m * 4 + b) * 80, preds[b])
        skill = sum(jnp.abs(p - truth) for p in preds) * 0.25
        spread = sum(
            jnp.abs(preds[b] - preds[c]) for b in range(4) for c in range(b + 1, 4)
        )
        put(crps_ref, m * 80, skill - spread * (1.0 / 12.0))


def run_net(pair, near, far, embed_w, merge_w, expand_w, head_w, fine_weight_kernels, coarse_w):
    params = pltpu.CompilerParams(vmem_limit_bytes=VMEM_LIMIT)
    vmem = pl.BlockSpec(memory_space=pltpu.VMEM)
    hbm = pl.BlockSpec(memory_space=pltpu.HBM)
    e_buf = pltpu.VMEM((40 * 32, 512), BF16)
    d_buf = pltpu.VMEM((36 * 32, 512), BF16)
    increments = pl.pallas_call(
        net_kernel,
        out_shape=jax.ShapeDtypeStruct((8, 16, 128), F32),
        in_specs=[vmem] * 3 + [hbm] * 6,
        out_specs=vmem,
        scratch_shapes=[
            pltpu.VMEM((2, 6912, 128), BF16),
            pltpu.VMEM((4, 6912, 256), BF16),
            pltpu.VMEM((7, 256), F32),
            pltpu.VMEM((512, 256), BF16),
            pltpu.VMEM((256, 512), BF16),
            pltpu.VMEM((5, 128), BF16),
            pltpu.VMEM((8, 256), F32),
            pltpu.VMEM((320, 128), F32),
            *[e_buf] * 4,
            *[d_buf] * 4,
            pltpu.VMEM((3, 576, 512), BF16),
            pltpu.VMEM((3, 576, 512), BF16),
            pltpu.SemaphoreType.DMA((10,)),
        ],
        compiler_params=params,
        name="net",
    )(pair, near, far, embed_w, merge_w, expand_w, head_w, fine_weight_kernels, coarse_w)
    return increments


def index(segment, column, z):
    return segment * TILES + column * GROUP + z


def body(
    state,
    noise,
    land_sea,
    observed_truth,
    embed_w,
    fine_weight_kernels,
    merge_w,
    coarse_w,
    expand_w,
    head_w,
):
    columns = TILES // GROUP
    state_rows = state.reshape(160, 64)
    vmem = pl.BlockSpec(memory_space=pltpu.VMEM)
    hbm = pl.BlockSpec(memory_space=pltpu.HBM)

    small = pltpu.CompilerParams(vmem_limit_bytes=SMALL_LIMIT)
    tile = jax.ShapeDtypeStruct((64, 128), F32)
    own, other = pl.pallas_call(
        pack_kernel,
        out_shape=(tile, tile),
        in_specs=[hbm] * 3,
        out_specs=(vmem, vmem),
        scratch_shapes=[
            pltpu.VMEM((160, 64), F32),
            pltpu.VMEM((2, 4, 2, 8, 64), F32),
            pltpu.VMEM((8, 64), jnp.int32),
            pltpu.VMEM((128, 64), F32),
            pltpu.VMEM((128, 64), F32),
            pltpu.SemaphoreType.DMA((3,)),
        ],
        compiler_params=small,
        name="pack",
    )(state_rows, noise, land_sea)

    every = [(s, c, z) for s in range(SEGMENTS) for c in range(columns) for z in range(GROUP)]
    beside = [(index(s, c, z), index(s, c, z ^ 1)) for s, c, z in every]
    across = [(index(s, c, z), index(s, c, z ^ 2)) for s, c, z in every]
    beyond = []
    for s, c, z in every:
        if c > 0 and z < 2:
            here, there = index(s, c, z), index(s ^ 2, c - 1, z + 2)
            beyond += [(here, there), (there, here)]

    got = lax.ppermute(other, AXES, beside)
    rows12 = jax.ShapeDtypeStruct((96, 128), F32)
    pair, near, far = pl.pallas_call(
        join_kernel,
        out_shape=(jax.ShapeDtypeStruct((128, 128), F32), rows12, rows12),
        in_specs=[vmem] * 2,
        out_specs=(vmem,) * 3,
        compiler_params=small,
        name="join",
    )(own, got)
    far = lax.ppermute(far, AXES, beyond)
    near = lax.ppermute(near, AXES, across)
    increments = run_net(
        pair, near, far, embed_w, merge_w, expand_w, head_w.T, fine_weight_kernels, coarse_w
    )

    squares = [
        [index(s, c, 2 * h + r) for s in range(SEGMENTS) for r in range(2)]
        for c in range(columns)
        for h in range(2)
    ]
    got = lax.all_to_all(increments, AXES, 0, 0, axis_index_groups=squares, tiled=True)

    prediction, crps = pl.pallas_call(
        score_kernel,
        out_shape=(
            jax.ShapeDtypeStruct((640, 16), F32),
            jax.ShapeDtypeStruct((160, 16), F32),
        ),
        in_specs=[vmem] * 3,
        out_specs=(vmem, vmem),
        compiler_params=small,
        name="score",
    )(got, state_rows, observed_truth.reshape(160, 16))
    return prediction.reshape(2, 4, 5, 2, 8, 16), crps.reshape(2, 5, 2, 8, 16)


def solution(mesh):
    return jax.shard_map(
        body,
        mesh=mesh,
        in_specs=(
            P(None, None, None, "space", None),
            P(None, None, None, "space", None),
            P("space", None),
            P(None, None, None, "space", "segment"),
            P(),
            P(),
            P(),
            P(),
            P(),
            P(),
        ),
        out_specs=(
            P(None, None, None, None, "space", "segment"),
            P(None, None, None, "space", "segment"),
        ),
        check_vma=False,
    )
```

```python
import jax
import jax.numpy as jnp
from jax import lax
from jax.experimental import pallas as pl
from jax.experimental.pallas import tpu as pltpu
from jax.sharding import PartitionSpec as P

F32 = jnp.float32
BF16 = jnp.bfloat16
AXES = ("segment", "space")
SEGMENTS = 4
TILES = 32
GROUP = 4
VMEM_LIMIT = 50 * 1024 * 1024
SMALL_LIMIT = 8 * 1024 * 1024
PACK_LIMIT = 60 * 1024 * 1024
R1 = 9
RC = 1
R2 = 4


def gelu(x):
    half = 0.5 * x
    t = jnp.tanh(x * (0.7978845608028654 + 0.035677408136300125 * (x * x)))
    return half + half * t


def nn(a, b):
    return lax.dot_general(a, b, (((1,), (0,)), ((), ())), preferred_element_type=F32)


def nt(a, b):
    return lax.dot_general(a, b, (((1,), (1,)), ((), ())), preferred_element_type=F32)


def iota(shape, dim):
    return lax.broadcasted_iota(jnp.int32, shape, dim)


def member_of(segment, space):
    return segment ^ (2 * ((space // GROUP) % 2))


def pack_kernel(
    state_hbm,
    noise_hbm,
    land_hbm,
    own_ref,
    other_ref,
    state_ref,
    noise_ref,
    land_ref,
    even_ref,
    odd_ref,
    sems,
):
    member = member_of(lax.axis_index("segment"), lax.axis_index("space"))
    copies = [
        pltpu.make_async_copy(state_hbm, state_ref, sems.at[0]),
        pltpu.make_async_copy(noise_hbm, noise_ref, sems.at[1]),
        pltpu.make_async_copy(land_hbm, land_ref, sems.at[2]),
    ]
    for copy in copies:
        copy.start()
    even_ref[...] = jnp.zeros_like(even_ref)
    odd_ref[...] = jnp.zeros_like(odd_ref)
    for copy in copies:
        copy.wait()
    for m in range(2):
        for lev in range(2):
            for y in range(8):
                dst = even_ref if y % 2 == 0 else odd_ref
                row = ((m * 4 + y // 2) * 2 + lev) * 8
                dst[pl.ds(row, 5), :] = state_ref[pl.ds(m * 80 + lev * 8 + y, 5, stride=16), :]
                dst[pl.ds(row + 5, 1), :] = noise_ref[m, member, lev, pl.ds(y, 1), :]
                dst[pl.ds(row + 6, 1), :] = land_ref[pl.ds(y, 1), :].astype(F32)
    total = jnp.zeros((128, 128), F32)
    for ylo, ref in ((0, even_ref), (1, odd_ref)):
        x = iota((64, 128), 0)
        lane = iota((64, 128), 1)
        spread = jnp.where(lane == (x % 2) * 64 + ylo * 32 + x // 2, 1.0, 0.0).astype(BF16)
        rest = ref[...]
        for _ in range(3):
            part = rest.astype(BF16)
            total = total + nn(part, spread)
            rest = rest - part.astype(F32)
    odd = lax.axis_index("space") % 2 == 1
    own_ref[...] = jnp.where(odd, total[64:], total[:64])
    other_ref[...] = jnp.where(odd, total[:64], total[64:])


def join_kernel(own_ref, got_ref, pair_ref, near_ref, far_ref):
    space = lax.axis_index("space")
    odd = space % 2 == 1
    upper = (space // 2) % 2 == 1
    pair_ref[pl.ds(0, 64), :] = jnp.where(odd, got_ref[...], own_ref[...])
    pair_ref[pl.ds(64, 64), :] = jnp.where(odd, own_ref[...], got_ref[...])
    head, tail = pair_ref[pl.ds(0, 96), :], pair_ref[pl.ds(32, 96), :]
    near_ref[...] = jnp.where(upper, head, tail)
    far_ref[...] = jnp.where(upper, tail, head)


def fetch_kernel(_, *refs):
    for src, dst in zip(refs[:4], refs[4:]):
        dst[...] = src[...]


def run_mask(v, row):
    runs = v.reshape(v.shape[0] // 32, 32, v.shape[1])
    return jnp.where(iota((1, 32, v.shape[1]), 1) != row, runs, 0.0).reshape(v.shape)


def shift_down(v):
    return run_mask(pltpu.roll(v, 1, 0), 0)


def shift_up(v):
    return run_mask(pltpu.roll(v, v.shape[0] - 1, 0), 31)


def net_kernel(
    pair_ref,
    near_ref,
    far_ref,
    embed_ref,
    merge_ref,
    expand_ref,
    head_ref,
    fine_hbm,
    coarse_hbm,
    out_ref,
    fine_w,
    coarse_w,
    ew_ref,
    f_ref,
    ee,
    eo,
    es1,
    es2,
    de,
    do,
    ds1,
    ds2,
    ca,
    cb,
    sems,
):
    space = lax.axis_index("space")
    upper = (space // 2) % 2 == 1
    first = space < 2
    last = space >= TILES - 2

    copies = [pltpu.make_async_copy(fine_hbm.at[0], fine_w.at[0], sems.at[0])]
    for k in range(4):
        copies.append(pltpu.make_async_copy(coarse_hbm.at[k], coarse_w.at[k], sems.at[1 + k]))
    copies.append(pltpu.make_async_copy(fine_hbm.at[1], fine_w.at[1], sems.at[5]))
    for copy in copies:
        copy.start()

    near, far = near_ref[...], far_ref[...]
    f_ref[pl.ds(0, 96), :] = jnp.where(upper, near, far)
    f_ref[pl.ds(96, 128), :] = pair_ref[...]
    f_ref[pl.ds(224, 96), :] = jnp.where(upper, far, near)

    ew_ref[...] = jnp.zeros_like(ew_ref)
    ew_ref[pl.ds(0, 7), :] = embed_ref[...]
    w = ew_ref[...]
    w_hi = w.astype(BF16).astype(F32)
    w_lo = w - w_hi
    w4 = jnp.concatenate([w_hi, w_hi, w_lo, w_lo], axis=0).astype(BF16)

    per = 10
    def embed_block(i, _):
        for lev in range(2):
            parts = []
            for j in range(per):
                t = f_ref[pl.ds(pl.multiple_of((i * per + j) * 16 + lev * 8, 8), 8), :]
                hi = t.astype(BF16).astype(F32)
                lo = t - hi
                parts.append(jnp.concatenate([hi, lo, hi, lo], axis=0).T)
            feats = jnp.concatenate(parts, axis=0).astype(BF16)
            g = gelu(nn(feats, w4))
            even = jnp.concatenate([g[j * 128 : j * 128 + 64] for j in range(per)], axis=0)
            odd = jnp.concatenate([g[j * 128 + 64 : j * 128 + 128] for j in range(per)], axis=0)
            rows = pl.ds(pl.multiple_of(i * per * 64, 64), per * 64)
            lanes = pl.ds(lev * 256, 256)
            ee[rows, lanes] = even.astype(BF16)
            eo[rows, lanes] = odd.astype(BF16)
            es1[rows, lanes] = shift_down(odd).astype(BF16)
            es2[rows, lanes] = shift_up(even).astype(BF16)
        return 0

    lax.fori_loop(0, 20 // per, embed_block, 0)

    def fine_conv(layer, row, n, srcs):
        e, o, s1, s2 = srcs
        sides = ((s1, e), (e, o), (o, s2))
        acc = None
        for dy in range(3):
            for dx in range(3):
                rows = pl.ds((row + dy) * 32, n * 32)
                a, b = sides[dx]
                lhs = jnp.concatenate([a[rows, :], b[rows, :]], axis=0)
                taps = [
                    fine_w[layer, pl.ds(((dz * 3 + dy) * 3 + dx) * 256, 256), :] for dz in range(3)
                ]
                rhs = jnp.concatenate(
                    [
                        jnp.concatenate([taps[1], taps[0]], axis=1),
                        jnp.concatenate([taps[2], taps[1]], axis=1),
                    ],
                    axis=0,
                )
                term = nn(lhs, rhs)
                acc = term if acc is None else acc + term
        return acc

    copies[0].wait()
    for blk in range(36 // R1):
        row = blk * R1
        g = gelu(fine_conv(0, row + 1, R1, (ee, eo, es1, es2)))
        even, odd = g[: R1 * 32], g[R1 * 32 :]
        rows = pl.ds(row * 32, R1 * 32)
        odd_s, even_s = shift_down(odd), shift_up(even)
        for lev in range(2):
            src = slice(lev * 128, lev * 128 + 128)
            dst = pl.ds(lev * 256 + 128, 128)
            de[rows, dst] = even[:, src].astype(BF16)
            do[rows, dst] = odd[:, src].astype(BF16)
            ds1[rows, dst] = odd_s[:, src].astype(BF16)
            ds2[rows, dst] = even_s[:, src].astype(BF16)

    @pl.when(first)
    def _():
        for ref in (de, do, ds1, ds2):
            ref[pl.ds(0, 320), :] = jnp.zeros((320, 512), BF16)

    @pl.when(last)
    def _():
        for ref in (de, do, ds1, ds2):
            ref[pl.ds(26 * 32, 320), :] = jnp.zeros((320, 512), BF16)

    def keep_coarse(dst, lev, v, start):
        lanes = pl.ds(lev * 256, 256)
        rows = pl.ds(start, v.shape[0])
        dst[1, rows, lanes] = v.astype(BF16)
        dst[0, rows, lanes] = shift_down(v).astype(BF16)
        dst[2, rows, lanes] = shift_up(v).astype(BF16)

    for lev in range(2):
        lanes = pl.ds(lev * 256 + 128, 128)
        pieces = [
            jnp.concatenate([ref[pl.ds((2 * r + dy) * 32, 32), lanes] for r in range(18)], axis=0)
            for dy in range(2)
            for ref in (de, do)
        ]
        keep_coarse(ca, lev, gelu(nn(jnp.concatenate(pieces, axis=1), merge_ref[...])), 0)

    src, dst = ca, cb
    for k in range(4):
        n = 16 - 2 * k
        copies[1 + k].wait()
        blocks = range(0, n, n // RC)
        for row in blocks:
            size = n // RC
            acc = [None, None]
            for dy in range(3):
                for dx in range(3):
                    lhs = src[dx, pl.ds((row + dy) * 32, size * 32), :]
                    taps = [
                        coarse_w[k, pl.ds(((dz * 3 + dy) * 3 + dx) * 256, 256), :]
                        for dz in range(3)
                    ]
                    for lev in range(2):
                        rhs = jnp.concatenate(
                            [taps[1], taps[2]] if lev == 0 else [taps[0], taps[1]], axis=0
                        )
                        term = nn(lhs, rhs)
                        acc[lev] = term if acc[lev] is None else acc[lev] + term
            for lev in range(2):
                before = src[1, pl.ds((row + 1) * 32, size * 32), pl.ds(lev * 256, 256)]
                keep_coarse(dst, lev, before.astype(F32) + gelu(acc[lev]), row * 32)
        edge = 4 - k

        @pl.when(first)
        def _(dst=dst, edge=edge):
            dst[:, pl.ds(0, edge * 32), :] = jnp.zeros((3, edge * 32, 512), BF16)

        @pl.when(last)
        def _(dst=dst, edge=edge, n=n):
            dst[:, pl.ds((n - edge) * 32, edge * 32), :] = jnp.zeros((3, edge * 32, 512), BF16)

        src, dst = dst, src

    for lev in range(2):
        up = nn(src[1, pl.ds(0, 320), pl.ds(lev * 256, 256)], expand_ref[...])
        lanes = pl.ds(lev * 256, 128)
        down, high = shift_down(up), shift_up(up)
        for d in range(18):
            r, dy = (d + 1) // 2, (d + 1) % 2
            rows = pl.ds((d + 9) * 32, 32)
            even = slice(dy * 256, dy * 256 + 128)
            odd = slice(dy * 256 + 128, dy * 256 + 256)
            here = slice(r * 32, r * 32 + 32)
            de[rows, lanes] = up[here, even].astype(BF16)
            do[rows, lanes] = up[here, odd].astype(BF16)
            ds1[rows, lanes] = down[here, odd].astype(BF16)
            ds2[rows, lanes] = high[here, even].astype(BF16)

    row_id = iota((16, 5), 0)
    var_id = iota((16, 5), 1)
    head = jnp.concatenate(
        [
            nn(jnp.where(row_id == 2 * var_id + lev, 1.0, 0.0).astype(BF16), head_ref[...])
            for lev in range(2)
        ],
        axis=1,
    ).astype(BF16)

    src_lane = iota((512, 1), 0)
    dst_lane = iota((512, 512), 1)
    lon = 2 * (src_lane & 31) + (src_lane >> 8)
    lat = (src_lane >> 5) & 7
    place = ((lon >> 4) << 7) + (lat << 4) + (lon & 15)
    spread = jnp.where(dst_lane == place, 1.0, 0.0).astype(BF16)

    copies[5].wait()
    for half in range(2):
        evens, odds = [], []
        for blk in range(8 // R2):
            row = half * 8 + blk * R2
            g = gelu(fine_conv(1, row + 9, R2, (de, do, ds1, ds2))).astype(BF16)
            evens.append(g[: R2 * 32])
            odds.append(g[R2 * 32 :])
        add = nt(head, jnp.concatenate(evens + odds, axis=0))
        hi = add.astype(BF16)
        lo = (add - hi.astype(F32)).astype(BF16)
        both = nn(jnp.concatenate([hi, lo], axis=0), spread)
        both = both[:16] + both[16:]
        for s in range(SEGMENTS):
            out_ref[s * 2 + half] = both[:, s * 128 : s * 128 + 128]


def score_kernel(got_ref, state_ref, truth_ref, pred_ref, crps_ref):
    segment = lax.axis_index("segment")
    space = lax.axis_index("space")
    lane = iota((10, 128), 1)

    def block_rows(ref, start, lanes_from):
        total = jnp.zeros((10, 128), F32)
        for y in range(8):
            v = ref[pl.ds(start + y, 10, stride=8), :]
            v = jnp.concatenate([v, jnp.zeros((10, 128 - v.shape[1]), F32)], axis=1)
            v = pltpu.roll(v, lax.rem(y * 16 - lanes_from + 128, 128), 1)
            total = jnp.where(lane // 16 == y, v, total)
        return total

    def put(ref, start, v):
        for y in range(8):
            w = pltpu.roll(v, (128 - 16 * y) % 128, 1) if y else v
            ref[pl.ds(start + y, 10, stride=8), :] = w[:, :16]

    for m in range(2):
        state = block_rows(state_ref, m * 80, segment * 16)
        truth = block_rows(truth_ref, m * 80, 0)
        preds = []
        for b in range(4):
            src = member_of(b, space) * 2 + m
            preds.append(got_ref[src][:10] + state)
            put(pred_ref, (m * 4 + b) * 80, preds[b])
        skill = sum(jnp.abs(p - truth) for p in preds) * 0.25
        spread = sum(
            jnp.abs(preds[b] - preds[c]) for b in range(4) for c in range(b + 1, 4)
        )
        put(crps_ref, m * 80, skill - spread * (1.0 / 12.0))


def run_net(pair, near, far, embed_w, merge_w, expand_w, head_w, fine_weight_kernels, coarse_w):
    params = pltpu.CompilerParams(vmem_limit_bytes=VMEM_LIMIT)
    vmem = pl.BlockSpec(memory_space=pltpu.VMEM)
    hbm = pl.BlockSpec(memory_space=pltpu.HBM)
    e_buf = pltpu.VMEM((40 * 32, 512), BF16)
    d_buf = pltpu.VMEM((36 * 32, 512), BF16)
    increments = pl.pallas_call(
        net_kernel,
        out_shape=jax.ShapeDtypeStruct((8, 16, 128), F32),
        in_specs=[vmem] * 7 + [hbm] * 2,
        out_specs=vmem,
        scratch_shapes=[
            pltpu.VMEM((2, 6912, 128), BF16),
            pltpu.VMEM((4, 6912, 256), BF16),
            pltpu.VMEM((8, 256), F32),
            pltpu.VMEM((320, 128), F32),
            *[e_buf] * 4,
            *[d_buf] * 4,
            pltpu.VMEM((3, 576, 512), BF16),
            pltpu.VMEM((3, 576, 512), BF16),
            pltpu.SemaphoreType.DMA((6,)),
        ],
        compiler_params=params,
        name="net",
    )(pair, near, far, embed_w, merge_w, expand_w, head_w, fine_weight_kernels, coarse_w)
    return increments


def index(segment, column, z):
    return segment * TILES + column * GROUP + z


def body(
    state,
    noise,
    land_sea,
    observed_truth,
    embed_w,
    fine_weight_kernels,
    merge_w,
    coarse_w,
    expand_w,
    head_w,
):
    columns = TILES // GROUP
    state_rows = state.reshape(160, 64)
    vmem = pl.BlockSpec(memory_space=pltpu.VMEM)
    hbm = pl.BlockSpec(memory_space=pltpu.HBM)

    small = pltpu.CompilerParams(vmem_limit_bytes=SMALL_LIMIT)
    tile = jax.ShapeDtypeStruct((64, 128), F32)
    own, other = pl.pallas_call(
        pack_kernel,
        out_shape=(tile, tile),
        in_specs=[hbm] * 3,
        out_specs=(vmem, vmem),
        scratch_shapes=[
            pltpu.VMEM((160, 64), F32),
            pltpu.VMEM((2, 4, 2, 8, 64), F32),
            pltpu.VMEM((8, 64), jnp.int32),
            pltpu.VMEM((128, 64), F32),
            pltpu.VMEM((128, 64), F32),
            pltpu.SemaphoreType.DMA((3,)),
        ],
        compiler_params=pltpu.CompilerParams(vmem_limit_bytes=PACK_LIMIT),
        name="pack",
    )(state_rows, noise, land_sea)

    every = [(s, c, z) for s in range(SEGMENTS) for c in range(columns) for z in range(GROUP)]
    beside = [(index(s, c, z), index(s, c, z ^ 1)) for s, c, z in every]
    across = [(index(s, c, z), index(s, c, z ^ 2)) for s, c, z in every]
    beyond = []
    for s, c, z in every:
        if c > 0 and z < 2:
            here, there = index(s, c, z), index(s ^ 2, c - 1, z + 2)
            beyond += [(here, there), (there, here)]

    got = lax.ppermute(other, AXES, beside)
    rows12 = jax.ShapeDtypeStruct((96, 128), F32)
    pair, near, far = pl.pallas_call(
        join_kernel,
        out_shape=(jax.ShapeDtypeStruct((128, 128), F32), rows12, rows12),
        in_specs=[vmem] * 2,
        out_specs=(vmem,) * 3,
        compiler_params=small,
        name="join",
    )(own, got)
    weights = (embed_w, merge_w, expand_w, head_w.T)
    embed_w, merge_w, expand_w, head_w = pl.pallas_call(
        fetch_kernel,
        out_shape=tuple(jax.ShapeDtypeStruct(w.shape, w.dtype) for w in weights),
        in_specs=[pl.BlockSpec(memory_space=pl.ANY)] + [vmem] * 4,
        out_specs=(vmem,) * 4,
        compiler_params=small,
        cost_estimate=pl.CostEstimate(flops=0, bytes_accessed=1 << 22, transcendentals=0),
        name="fetch",
    )(pair, *weights)
    far = lax.ppermute(far, AXES, beyond)
    near = lax.ppermute(near, AXES, across)
    increments = run_net(
        pair, near, far, embed_w, merge_w, expand_w, head_w, fine_weight_kernels, coarse_w
    )

    squares = [
        [index(s, c, 2 * h + r) for s in range(SEGMENTS) for r in range(2)]
        for c in range(columns)
        for h in range(2)
    ]
    got = lax.all_to_all(increments, AXES, 0, 0, axis_index_groups=squares, tiled=True)

    prediction, crps = pl.pallas_call(
        score_kernel,
        out_shape=(
            jax.ShapeDtypeStruct((640, 16), F32),
            jax.ShapeDtypeStruct((160, 16), F32),
        ),
        in_specs=[vmem] * 3,
        out_specs=(vmem, vmem),
        compiler_params=small,
        name="score",
    )(got, state_rows, observed_truth.reshape(160, 16))
    return prediction.reshape(2, 4, 5, 2, 8, 16), crps.reshape(2, 5, 2, 8, 16)


def solution(mesh):
    return jax.shard_map(
        body,
        mesh=mesh,
        in_specs=(
            P(None, None, None, "space", None),
            P(None, None, None, "space", None),
            P("space", None),
            P(None, None, None, "space", "segment"),
            P(),
            P(),
            P(),
            P(),
            P(),
            P(),
        ),
        out_specs=(
            P(None, None, None, None, "space", "segment"),
            P(None, None, None, "space", "segment"),
        ),
        check_vma=False,
    )
```

```python
import jax
import jax.numpy as jnp
from jax import lax
from jax.experimental import pallas as pl
from jax.experimental.pallas import tpu as pltpu
from jax.sharding import PartitionSpec as P

F32 = jnp.float32
BF16 = jnp.bfloat16
AXES = ("segment", "space")
SEGMENTS = 4
TILES = 32
GROUP = 4
VMEM_LIMIT = 50 * 1024 * 1024
SMALL_LIMIT = 8 * 1024 * 1024
PACK_LIMIT = 60 * 1024 * 1024
R1 = 9
RC = 1
R2 = 4


def gelu(x):
    half = 0.5 * x
    t = jnp.tanh(x * (0.7978845608028654 + 0.035677408136300125 * (x * x)))
    return half + half * t


def nn(a, b):
    return lax.dot_general(a, b, (((1,), (0,)), ((), ())), preferred_element_type=F32)


def nt(a, b):
    return lax.dot_general(a, b, (((1,), (1,)), ((), ())), preferred_element_type=F32)


def iota(shape, dim):
    return lax.broadcasted_iota(jnp.int32, shape, dim)


def member_of(segment, space):
    return segment ^ (2 * ((space // GROUP) % 2))


def pack_kernel(
    state_hbm,
    noise_hbm,
    land_hbm,
    own_ref,
    other_ref,
    state_ref,
    noise_ref,
    land_ref,
    even_ref,
    odd_ref,
    sems,
):
    member = member_of(lax.axis_index("segment"), lax.axis_index("space"))
    copies = [
        pltpu.make_async_copy(state_hbm, state_ref, sems.at[0]),
        pltpu.make_async_copy(noise_hbm, noise_ref, sems.at[1]),
        pltpu.make_async_copy(land_hbm, land_ref, sems.at[2]),
    ]
    for copy in copies:
        copy.start()
    even_ref[...] = jnp.zeros_like(even_ref)
    odd_ref[...] = jnp.zeros_like(odd_ref)
    for copy in copies:
        copy.wait()
    for m in range(2):
        for lev in range(2):
            for y in range(8):
                dst = even_ref if y % 2 == 0 else odd_ref
                row = ((m * 4 + y // 2) * 2 + lev) * 8
                dst[pl.ds(row, 5), :] = state_ref[pl.ds(m * 80 + lev * 8 + y, 5, stride=16), :]
                dst[pl.ds(row + 5, 1), :] = noise_ref[m, member, lev, pl.ds(y, 1), :]
                dst[pl.ds(row + 6, 1), :] = land_ref[pl.ds(y, 1), :].astype(F32)
    total = jnp.zeros((128, 128), F32)
    for ylo, ref in ((0, even_ref), (1, odd_ref)):
        x = iota((64, 128), 0)
        lane = iota((64, 128), 1)
        spread = jnp.where(lane == (x % 2) * 64 + ylo * 32 + x // 2, 1.0, 0.0).astype(BF16)
        rest = ref[...]
        for _ in range(3):
            part = rest.astype(BF16)
            total = total + nn(part, spread)
            rest = rest - part.astype(F32)
    odd = lax.axis_index("space") % 2 == 1
    own_ref[...] = jnp.where(odd, total[64:], total[:64])
    other_ref[...] = jnp.where(odd, total[:64], total[64:])


def join_kernel(own_ref, got_ref, pair_ref, near_ref, far_ref):
    space = lax.axis_index("space")
    odd = space % 2 == 1
    upper = (space // 2) % 2 == 1
    pair_ref[pl.ds(0, 64), :] = jnp.where(odd, got_ref[...], own_ref[...])
    pair_ref[pl.ds(64, 64), :] = jnp.where(odd, own_ref[...], got_ref[...])
    head, tail = pair_ref[pl.ds(0, 96), :], pair_ref[pl.ds(32, 96), :]
    near_ref[...] = jnp.where(upper, head, tail)
    far_ref[...] = jnp.where(upper, tail, head)


def fetch_kernel(
    _,
    embed_ref,
    merge_in,
    expand_in,
    head_ref,
    w4_ref,
    merge_out,
    expand_out,
    row_ref,
    spread_ref,
    ew_ref,
):
    merge_out[...] = merge_in[...]
    expand_out[...] = expand_in[...]
    ew_ref[...] = jnp.zeros_like(ew_ref)
    ew_ref[pl.ds(0, 7), :] = embed_ref[...]
    w = ew_ref[...]
    w_hi = w.astype(BF16).astype(F32)
    w_lo = w - w_hi
    w4_ref[...] = jnp.concatenate([w_hi, w_hi, w_lo, w_lo], axis=0).astype(BF16)
    row_id = iota((16, 5), 0)
    var_id = iota((16, 5), 1)
    row_ref[...] = jnp.concatenate(
        [
            nn(jnp.where(row_id == 2 * var_id + lev, 1.0, 0.0).astype(BF16), head_ref[...])
            for lev in range(2)
        ],
        axis=1,
    ).astype(BF16)

    src_lane = iota((512, 1), 0)
    dst_lane = iota((512, 512), 1)
    lon = 2 * (src_lane & 31) + (src_lane >> 8)
    lat = (src_lane >> 5) & 7
    place = ((lon >> 4) << 7) + (lat << 4) + (lon & 15)
    spread_ref[...] = jnp.where(dst_lane == place, 1.0, 0.0).astype(BF16)


def run_mask(v, row):
    runs = v.reshape(v.shape[0] // 32, 32, v.shape[1])
    return jnp.where(iota((1, 32, v.shape[1]), 1) != row, runs, 0.0).reshape(v.shape)


def shift_down(v):
    return run_mask(pltpu.roll(v, 1, 0), 0)


def shift_up(v):
    return run_mask(pltpu.roll(v, v.shape[0] - 1, 0), 31)


def net_kernel(
    pair_ref,
    near_ref,
    far_ref,
    embed_ref,
    merge_ref,
    expand_ref,
    head_ref,
    spread_ref,
    fine_hbm,
    coarse_hbm,
    out_ref,
    fine_w,
    coarse_w,
    f_ref,
    ee,
    eo,
    es1,
    es2,
    de,
    do,
    ds1,
    ds2,
    ca,
    cb,
    sems,
):
    space = lax.axis_index("space")
    upper = (space // 2) % 2 == 1
    first = space < 2
    last = space >= TILES - 2

    copies = [pltpu.make_async_copy(fine_hbm.at[0], fine_w.at[0], sems.at[0])]
    for k in range(4):
        copies.append(pltpu.make_async_copy(coarse_hbm.at[k], coarse_w.at[k], sems.at[1 + k]))
    copies.append(pltpu.make_async_copy(fine_hbm.at[1], fine_w.at[1], sems.at[5]))
    for copy in copies:
        copy.start()

    near, far = near_ref[...], far_ref[...]
    f_ref[pl.ds(0, 96), :] = jnp.where(upper, near, far)
    f_ref[pl.ds(96, 128), :] = pair_ref[...]
    f_ref[pl.ds(224, 96), :] = jnp.where(upper, far, near)

    w4 = embed_ref[...]
    per = 10
    def embed_block(i, _):
        for lev in range(2):
            parts = []
            for j in range(per):
                t = f_ref[pl.ds(pl.multiple_of((i * per + j) * 16 + lev * 8, 8), 8), :]
                hi = t.astype(BF16).astype(F32)
                lo = t - hi
                parts.append(jnp.concatenate([hi, lo, hi, lo], axis=0).T)
            feats = jnp.concatenate(parts, axis=0).astype(BF16)
            g = gelu(nn(feats, w4))
            even = jnp.concatenate([g[j * 128 : j * 128 + 64] for j in range(per)], axis=0)
            odd = jnp.concatenate([g[j * 128 + 64 : j * 128 + 128] for j in range(per)], axis=0)
            rows = pl.ds(pl.multiple_of(i * per * 64, 64), per * 64)
            lanes = pl.ds(lev * 256, 256)
            ee[rows, lanes] = even.astype(BF16)
            eo[rows, lanes] = odd.astype(BF16)
            es1[rows, lanes] = shift_down(odd).astype(BF16)
            es2[rows, lanes] = shift_up(even).astype(BF16)
        return 0

    lax.fori_loop(0, 20 // per, embed_block, 0)

    def fine_conv(layer, row, n, srcs):
        e, o, s1, s2 = srcs
        sides = ((s1, e), (e, o), (o, s2))
        acc = None
        for dy in range(3):
            for dx in range(3):
                rows = pl.ds((row + dy) * 32, n * 32)
                a, b = sides[dx]
                lhs = jnp.concatenate([a[rows, :], b[rows, :]], axis=0)
                taps = [
                    fine_w[layer, pl.ds(((dz * 3 + dy) * 3 + dx) * 256, 256), :] for dz in range(3)
                ]
                rhs = jnp.concatenate(
                    [
                        jnp.concatenate([taps[1], taps[0]], axis=1),
                        jnp.concatenate([taps[2], taps[1]], axis=1),
                    ],
                    axis=0,
                )
                term = nn(lhs, rhs)
                acc = term if acc is None else acc + term
        return acc

    copies[0].wait()
    for blk in range(36 // R1):
        row = blk * R1
        g = gelu(fine_conv(0, row + 1, R1, (ee, eo, es1, es2)))
        even, odd = g[: R1 * 32], g[R1 * 32 :]
        rows = pl.ds(row * 32, R1 * 32)
        odd_s, even_s = shift_down(odd), shift_up(even)
        for lev in range(2):
            src = slice(lev * 128, lev * 128 + 128)
            dst = pl.ds(lev * 256 + 128, 128)
            de[rows, dst] = even[:, src].astype(BF16)
            do[rows, dst] = odd[:, src].astype(BF16)
            ds1[rows, dst] = odd_s[:, src].astype(BF16)
            ds2[rows, dst] = even_s[:, src].astype(BF16)

    @pl.when(first)
    def _():
        for ref in (de, do, ds1, ds2):
            ref[pl.ds(0, 320), :] = jnp.zeros((320, 512), BF16)

    @pl.when(last)
    def _():
        for ref in (de, do, ds1, ds2):
            ref[pl.ds(26 * 32, 320), :] = jnp.zeros((320, 512), BF16)

    def keep_coarse(dst, lev, v, start):
        lanes = pl.ds(lev * 256, 256)
        rows = pl.ds(start, v.shape[0])
        dst[1, rows, lanes] = v.astype(BF16)
        dst[0, rows, lanes] = shift_down(v).astype(BF16)
        dst[2, rows, lanes] = shift_up(v).astype(BF16)

    for lev in range(2):
        lanes = pl.ds(lev * 256 + 128, 128)
        pieces = [
            jnp.concatenate([ref[pl.ds((2 * r + dy) * 32, 32), lanes] for r in range(18)], axis=0)
            for dy in range(2)
            for ref in (de, do)
        ]
        keep_coarse(ca, lev, gelu(nn(jnp.concatenate(pieces, axis=1), merge_ref[...])), 0)

    src, dst = ca, cb
    for k in range(4):
        n = 16 - 2 * k
        copies[1 + k].wait()
        blocks = range(0, n, n // RC)
        for row in blocks:
            size = n // RC
            acc = [None, None]
            for dy in range(3):
                for dx in range(3):
                    lhs = src[dx, pl.ds((row + dy) * 32, size * 32), :]
                    taps = [
                        coarse_w[k, pl.ds(((dz * 3 + dy) * 3 + dx) * 256, 256), :]
                        for dz in range(3)
                    ]
                    for lev in range(2):
                        rhs = jnp.concatenate(
                            [taps[1], taps[2]] if lev == 0 else [taps[0], taps[1]], axis=0
                        )
                        term = nn(lhs, rhs)
                        acc[lev] = term if acc[lev] is None else acc[lev] + term
            for lev in range(2):
                before = src[1, pl.ds((row + 1) * 32, size * 32), pl.ds(lev * 256, 256)]
                keep_coarse(dst, lev, before.astype(F32) + gelu(acc[lev]), row * 32)
        edge = 4 - k

        @pl.when(first)
        def _(dst=dst, edge=edge):
            dst[:, pl.ds(0, edge * 32), :] = jnp.zeros((3, edge * 32, 512), BF16)

        @pl.when(last)
        def _(dst=dst, edge=edge, n=n):
            dst[:, pl.ds((n - edge) * 32, edge * 32), :] = jnp.zeros((3, edge * 32, 512), BF16)

        src, dst = dst, src

    for lev in range(2):
        up = nn(src[1, pl.ds(0, 320), pl.ds(lev * 256, 256)], expand_ref[...])
        lanes = pl.ds(lev * 256, 128)
        down, high = shift_down(up), shift_up(up)
        for d in range(18):
            r, dy = (d + 1) // 2, (d + 1) % 2
            rows = pl.ds((d + 9) * 32, 32)
            even = slice(dy * 256, dy * 256 + 128)
            odd = slice(dy * 256 + 128, dy * 256 + 256)
            here = slice(r * 32, r * 32 + 32)
            de[rows, lanes] = up[here, even].astype(BF16)
            do[rows, lanes] = up[here, odd].astype(BF16)
            ds1[rows, lanes] = down[here, odd].astype(BF16)
            ds2[rows, lanes] = high[here, even].astype(BF16)

    head, spread = head_ref[...], spread_ref[...]
    copies[5].wait()
    for half in range(2):
        evens, odds = [], []
        for blk in range(8 // R2):
            row = half * 8 + blk * R2
            g = gelu(fine_conv(1, row + 9, R2, (de, do, ds1, ds2))).astype(BF16)
            evens.append(g[: R2 * 32])
            odds.append(g[R2 * 32 :])
        add = nt(head, jnp.concatenate(evens + odds, axis=0))
        hi = add.astype(BF16)
        lo = (add - hi.astype(F32)).astype(BF16)
        both = nn(jnp.concatenate([hi, lo], axis=0), spread)
        both = both[:16] + both[16:]
        for s in range(SEGMENTS):
            out_ref[s * 2 + half] = both[:, s * 128 : s * 128 + 128]


def score_kernel(got_ref, state_ref, truth_ref, pred_ref, crps_ref):
    segment = lax.axis_index("segment")
    space = lax.axis_index("space")
    lane = iota((10, 128), 1)

    def block_rows(ref, start, lanes_from):
        total = jnp.zeros((10, 128), F32)
        for y in range(8):
            v = ref[pl.ds(start + y, 10, stride=8), :]
            v = jnp.concatenate([v, jnp.zeros((10, 128 - v.shape[1]), F32)], axis=1)
            v = pltpu.roll(v, lax.rem(y * 16 - lanes_from + 128, 128), 1)
            total = jnp.where(lane // 16 == y, v, total)
        return total

    def put(ref, start, v):
        for y in range(8):
            w = pltpu.roll(v, (128 - 16 * y) % 128, 1) if y else v
            ref[pl.ds(start + y, 10, stride=8), :] = w[:, :16]

    for m in range(2):
        state = block_rows(state_ref, m * 80, segment * 16)
        truth = block_rows(truth_ref, m * 80, 0)
        preds = []
        for b in range(4):
            src = member_of(b, space) * 2 + m
            preds.append(got_ref[src][:10] + state)
            put(pred_ref, (m * 4 + b) * 80, preds[b])
        skill = sum(jnp.abs(p - truth) for p in preds) * 0.25
        spread = sum(
            jnp.abs(preds[b] - preds[c]) for b in range(4) for c in range(b + 1, 4)
        )
        put(crps_ref, m * 80, skill - spread * (1.0 / 12.0))


def run_net(pair, near, far, w4, merge_w, expand_w, head, spread, fine_weight_kernels, coarse_w):
    params = pltpu.CompilerParams(vmem_limit_bytes=VMEM_LIMIT)
    vmem = pl.BlockSpec(memory_space=pltpu.VMEM)
    hbm = pl.BlockSpec(memory_space=pltpu.HBM)
    e_buf = pltpu.VMEM((40 * 32, 512), BF16)
    d_buf = pltpu.VMEM((36 * 32, 512), BF16)
    increments = pl.pallas_call(
        net_kernel,
        out_shape=jax.ShapeDtypeStruct((8, 16, 128), F32),
        in_specs=[vmem] * 8 + [hbm] * 2,
        out_specs=vmem,
        scratch_shapes=[
            pltpu.VMEM((2, 6912, 128), BF16),
            pltpu.VMEM((4, 6912, 256), BF16),
            pltpu.VMEM((320, 128), F32),
            *[e_buf] * 4,
            *[d_buf] * 4,
            pltpu.VMEM((3, 576, 512), BF16),
            pltpu.VMEM((3, 576, 512), BF16),
            pltpu.SemaphoreType.DMA((6,)),
        ],
        compiler_params=params,
        name="net",
    )(pair, near, far, w4, merge_w, expand_w, head, spread, fine_weight_kernels, coarse_w)
    return increments


def index(segment, column, z):
    return segment * TILES + column * GROUP + z


def body(
    state,
    noise,
    land_sea,
    observed_truth,
    embed_w,
    fine_weight_kernels,
    merge_w,
    coarse_w,
    expand_w,
    head_w,
):
    columns = TILES // GROUP
    state_rows = state.reshape(160, 64)
    vmem = pl.BlockSpec(memory_space=pltpu.VMEM)
    hbm = pl.BlockSpec(memory_space=pltpu.HBM)

    small = pltpu.CompilerParams(vmem_limit_bytes=SMALL_LIMIT)
    tile = jax.ShapeDtypeStruct((64, 128), F32)
    own, other = pl.pallas_call(
        pack_kernel,
        out_shape=(tile, tile),
        in_specs=[hbm] * 3,
        out_specs=(vmem, vmem),
        scratch_shapes=[
            pltpu.VMEM((160, 64), F32),
            pltpu.VMEM((2, 4, 2, 8, 64), F32),
            pltpu.VMEM((8, 64), jnp.int32),
            pltpu.VMEM((128, 64), F32),
            pltpu.VMEM((128, 64), F32),
            pltpu.SemaphoreType.DMA((3,)),
        ],
        compiler_params=pltpu.CompilerParams(vmem_limit_bytes=PACK_LIMIT),
        name="pack",
    )(state_rows, noise, land_sea)

    every = [(s, c, z) for s in range(SEGMENTS) for c in range(columns) for z in range(GROUP)]
    beside = [(index(s, c, z), index(s, c, z ^ 1)) for s, c, z in every]
    across = [(index(s, c, z), index(s, c, z ^ 2)) for s, c, z in every]
    beyond = []
    for s, c, z in every:
        if c > 0 and z < 2:
            here, there = index(s, c, z), index(s ^ 2, c - 1, z + 2)
            beyond += [(here, there), (there, here)]

    got = lax.ppermute(other, AXES, beside)
    rows12 = jax.ShapeDtypeStruct((96, 128), F32)
    pair, near, far = pl.pallas_call(
        join_kernel,
        out_shape=(jax.ShapeDtypeStruct((128, 128), F32), rows12, rows12),
        in_specs=[vmem] * 2,
        out_specs=(vmem,) * 3,
        compiler_params=small,
        name="join",
    )(own, got)
    made = ((32, 256), merge_w.shape, expand_w.shape, (16, 256), (512, 512))
    w4, merge_w, expand_w, head, spread = pl.pallas_call(
        fetch_kernel,
        out_shape=tuple(jax.ShapeDtypeStruct(shape, BF16) for shape in made),
        in_specs=[pl.BlockSpec(memory_space=pl.ANY)] + [vmem] * 4,
        out_specs=(vmem,) * 5,
        scratch_shapes=[pltpu.VMEM((8, 256), F32)],
        compiler_params=small,
        cost_estimate=pl.CostEstimate(flops=0, bytes_accessed=1 << 22, transcendentals=0),
        name="fetch",
    )(pair, embed_w, merge_w, expand_w, head_w.T)
    far = lax.ppermute(far, AXES, beyond)
    near = lax.ppermute(near, AXES, across)
    increments = run_net(
        pair, near, far, w4, merge_w, expand_w, head, spread, fine_weight_kernels, coarse_w
    )

    squares = [
        [index(s, c, 2 * h + r) for s in range(SEGMENTS) for r in range(2)]
        for c in range(columns)
        for h in range(2)
    ]
    got = lax.all_to_all(increments, AXES, 0, 0, axis_index_groups=squares, tiled=True)

    prediction, crps = pl.pallas_call(
        score_kernel,
        out_shape=(
            jax.ShapeDtypeStruct((640, 16), F32),
            jax.ShapeDtypeStruct((160, 16), F32),
        ),
        in_specs=[vmem] * 3,
        out_specs=(vmem, vmem),
        compiler_params=small,
        name="score",
    )(got, state_rows, observed_truth.reshape(160, 16))
    return prediction.reshape(2, 4, 5, 2, 8, 16), crps.reshape(2, 5, 2, 8, 16)


def solution(mesh):
    return jax.shard_map(
        body,
        mesh=mesh,
        in_specs=(
            P(None, None, None, "space", None),
            P(None, None, None, "space", None),
            P("space", None),
            P(None, None, None, "space", "segment"),
            P(),
            P(),
            P(),
            P(),
            P(),
            P(),
        ),
        out_specs=(
            P(None, None, None, None, "space", "segment"),
            P(None, None, None, "space", "segment"),
        ),
        check_vma=False,
    )
```
